256 devices in a mesh: segment: 2 (over x_lo), expert: 128 (over y, x_hi, z, core).
Axes of the slice: x: 4 (x_hi: 2, x_lo: 2; x = x_hi * 2 + x_lo), y: 4, z: 8, core: 2. Of those that a mesh axis runs over, the one named last changes fastest.
Arguments:
- boundary: bfloat16 [2, 8192, 2048], P('segment', 'expert'), may hold values from -6 to 6
- saved: bfloat16 [2, 8192, 2048], P('segment', 'expert'), may hold values from -6 to 6
- norm_gain: float32 [2, 2048], P('segment'), may hold values from 0.25 to 1.75
- gate_weight: bfloat16 [2, 128, 2048, 768], P('segment', 'expert'), may hold values from -0.125 to 0.125
- up_weight: bfloat16 [2, 128, 2048, 768], P('segment', 'expert'), may hold values from -0.125 to 0.125
- down_weight: bfloat16 [2, 128, 768, 2048], P('segment', 'expert'), may hold values from -0.21875 to 0.21875
- routes: int32 [2, 2, 8192, 8], P('segment', None, 'expert'), may hold values from 0 to 127, all different within a row; in each aligned block of 64 rows (0 to 63, 64 to 127, ..., all dimensions but the last counted through in order) at most 6 rows name the same one
- gate_codes: int32 [2, 2, 8192, 8], P('segment', None, 'expert'), may hold values from 1 to 16
Outputs:
- results: bfloat16 [2, 8192, 2048], P('segment', 'expert')
The draws below stay inside these ranges and needn't reach their ends.
Inputs may be any that keep to these rules, and one draw needn't show every extreme that they name: `routes`: each row names 8 different experts. Among the rows of one index of expert (aligned blocks of 64 rows) no expert is named by more than 6 rows, a bound that some block reaches.
All inputs are finite; a program needn't handle non-finite values.
Results may differ from the reference program's by a relative error of at most 0.0075.
Values may be sent and summed in bfloat16 or wider, within the bound.
No kernel may reach another device: no remote copies, remote signals or barrier semaphores. Data moves between devices by JAX's collectives and lax.ppermute only.
A program may use at most 128 MiB of HBM per device.

```python
import math
import jax
import jax.numpy as jnp
import numpy as np
from jax import lax

D = 2048
FF = 768
TOP = 8
EXPERTS = 128
TOK_DEV = 64
TOKENS = 8192
CAP = 6
N_EXPERT = 128


def set_ends(drawn, rng, least, largest):
    index_at = [jax.random.randint(jax.random.fold_in(rng, axis), (), 0, length) for axis, length in enumerate(drawn.shape)]
    main_axis = drawn.shape.index(max(drawn.shape))
    beside = index_at[:main_axis] + [(index_at[main_axis] + 1) % drawn.shape[main_axis]] + index_at[main_axis + 1:]
    return drawn.at[tuple(index_at)].set(least).at[tuple(beside)].set(largest)


def block_levels(own_key, dims, cuts, smallest, largest):
    factor_of, own = 1.0, jax.random.fold_in(own_key, 6)
    for axis_at, shards_of in cuts:
        heights = jnp.exp(jax.random.uniform(jax.random.fold_in(own, axis_at), (shards_of,), jnp.float32, smallest / len(cuts), largest / len(cuts)))
        factor_of = factor_of * jnp.repeat(heights, dims[axis_at] // shards_of).reshape([-1 if axis == axis_at else 1 for axis in range(len(dims))])
    return factor_of


def assign_block(stream_key, own, number, rows, number_of, top, limit, skew):
    sequence = jax.random.permutation(stream_key, number_of)
    heavy_load, common = shares(number_of, rows * top, limit, skew, True), shares(number_of, rows * top, limit, skew, False)
    places = jnp.arange(number_of)

    def named(tallies, turn):
        used = int((tallies > 0).sum())
        fixed = max(1, used // 4)
        moved = fixed + (places - fixed + turn * (used - fixed)) % max(1, number_of - fixed)
        return jnp.zeros((number_of,), jnp.int32).at[sequence[jnp.where(places < fixed, places, moved)]].set(jnp.asarray(tallies, jnp.int32))

    tallies = jnp.where(number % 4 == 0, named(heavy_load, number // 4), named(common, number - number // 4 - 1))
    mixed = jax.random.permutation(jax.random.fold_in(own, 3), number_of)
    source_of, taker = mixed[0:number_of // 2 * 2:2], mixed[1:number_of // 2 * 2:2]
    room = jnp.minimum(tallies[source_of] - 1, limit - tallies[taker]) // 2
    room = jnp.where((source_of == sequence[0]) | (taker == sequence[0]) | (tallies[taker] == 0), 0, jnp.maximum(room, 0))
    moved = jax.random.randint(jax.random.fold_in(own, 4), (number_of // 2,), 0, 1 << 20) % (room + 1)
    tallies = tallies.at[source_of].add(-moved).at[taker].add(moved)
    members = jnp.searchsorted(jnp.cumsum(tallies), jnp.arange(rows * top), side="right").astype(jnp.int32)
    grid = members.reshape(top, rows).T
    grid = grid[jax.random.permutation(jax.random.fold_in(own, 1), rows)]
    turn = jax.random.randint(jax.random.fold_in(own, 2), (rows, 1), 0, top)
    return jnp.take_along_axis(grid, (jnp.arange(top)[None, :] + turn) % top, axis=1)


def shares(count, total, most, skew, full):
    portions = [(1 << 20) // math.isqrt(standing ** skew) + 1 for standing in range(1, count + 1)]
    largest = most if full else min(most, max(-(-total // count), total * portions[0] // sum(portions)))
    least = 1 if total - largest >= count - 1 else 0
    counts, surplus = [largest] + [least] * (count - 1), total - largest - least * (count - 1)
    while surplus > 0:
        movable = [i for i in range(1, count) if counts[i] < largest] or [i for i in range(1, count) if counts[i] < most]
        whole, remaining = sum([portions[i] for i in movable]), surplus
        for i in movable:
            extra = min(most - counts[i], max(1, remaining * portions[i] // whole), surplus)
            counts[i] = counts[i] + extra
            surplus = surplus - extra
    return np.array(counts)


def centred(key, extent, width, limit, split=(), held_as=jnp.bfloat16):
    factor_of = block_levels(key, extent, split, -0.22, 0.18) if split else 1.0
    result = jax.random.normal(key, extent, jnp.float32) * width * factor_of
    return jnp.minimum(jnp.maximum(result, -limit), limit).astype(held_as)


def setup_inputs(seed: int = 0) -> dict:
    streams_of = jax.random.split(jax.random.key(seed), 9)
    boundary = centred(streams_of[0], (2, TOKENS, D), 1.0, 6.0, ((0, 2), (1, 128)))
    saved = centred(streams_of[1], (2, TOKENS, D), 1.0, 6.0, ((0, 2), (1, 128)))
    norm_gain = jnp.clip(1.0 + 0.15 * jax.random.normal(streams_of[2], (2, D), jnp.float32), 0.25, 1.75)
    gate_weight = centred(streams_of[3], (2, EXPERTS, D, FF), D ** -0.5, 0.125, ((0, 2), (1, 128)))
    up_weight = centred(streams_of[4], (2, EXPERTS, D, FF), D ** -0.5, 0.125, ((0, 2), (1, 128)))
    down_weight = centred(streams_of[5], (2, EXPERTS, FF, D), FF ** -0.5, 0.21875, ((0, 2), (1, 128)))
    routes_keys = jax.random.split(jax.random.fold_in(streams_of[6], 1), 2 * 2 * TOKENS // TOK_DEV)
    routes_turns = jax.random.permutation(jax.random.fold_in(streams_of[6], 3), 2 * 2 * TOKENS // TOK_DEV)
    routes = jax.vmap(lambda own, number: assign_block(jax.random.fold_in(streams_of[6], 2), own, number, TOK_DEV, EXPERTS, TOP, CAP, 2))(routes_keys, routes_turns).reshape((2, 2, TOKENS, TOP))
    gate_codes = set_ends(jax.random.randint(streams_of[7], (2, 2, TOKENS, TOP), 1, 17), jax.random.fold_in(streams_of[7], 1), 1, 16).astype(jnp.int32)
    return dict(boundary=boundary, saved=saved, norm_gain=norm_gain, gate_weight=gate_weight, up_weight=up_weight, down_weight=down_weight, routes=routes, gate_codes=gate_codes)


epsilon = 1e-06

def gate_values(codes):
    counted = codes.astype(jnp.float32)
    return counted / lax.optimization_barrier(jnp.sum(counted, axis=-1, keepdims=True))

def normalize(inputs, gain_row):
    widened = inputs.astype(jnp.float32)
    scaling = lax.rsqrt(lax.optimization_barrier(jnp.mean(widened * widened, axis=-1, keepdims=True)) + epsilon)
    return (widened, scaling, (widened * scaling * gain_row).astype(jnp.bfloat16))

def transposed(left, right):
    return lax.dot_general(left, right, (((1,), (1,)), ((), ())), preferred_element_type=jnp.float32)

def expert_forward(row_block, w_gate, w_up, w_down):
    gate_part = jnp.dot(row_block, w_gate, preferred_element_type=jnp.float32)
    up_part = jnp.dot(row_block, w_up, preferred_element_type=jnp.float32)
    hidden = (gate_part * jax.nn.sigmoid(gate_part) * up_part).astype(jnp.bfloat16)
    return jnp.dot(hidden, w_down, preferred_element_type=jnp.float32).astype(jnp.bfloat16)

def expert_backward(row_block, grad_block, w_gate, w_up, w_down):
    gate_part = jnp.dot(row_block, w_gate, preferred_element_type=jnp.float32)
    up_part = jnp.dot(row_block, w_up, preferred_element_type=jnp.float32)
    sigmoid_part = jax.nn.sigmoid(gate_part)
    activated = gate_part * sigmoid_part
    slope = sigmoid_part * (1.0 + gate_part * (1.0 - sigmoid_part))
    hidden_grad = transposed(grad_block, w_down)
    gate_grad = (hidden_grad * up_part * slope).astype(jnp.bfloat16)
    up_grad = (hidden_grad * activated).astype(jnp.bfloat16)
    return (transposed(gate_grad, w_gate) + transposed(up_grad, w_up)).astype(jnp.bfloat16)

def expert_sums(route, gates, operands, weights, kernel):
    flat_ids = route.reshape(-1).astype(jnp.int32)
    assign_count = TOKENS * TOP
    slot_count = N_EXPERT * CAP
    assign_ids = jnp.arange(assign_count, dtype=jnp.int32)

    def one_expert(packed):
        expert_id, w_gate, w_up, w_down = packed
        matched = flat_ids == expert_id
        position = jnp.cumsum(matched.astype(jnp.int32)) - 1
        target = jnp.where(matched, position, slot_count).astype(jnp.int32)
        taken_ids = jnp.full((slot_count,), assign_count, jnp.int32).at[target].set(assign_ids, mode='drop')
        token_ids = jnp.minimum(taken_ids // TOP, TOKENS - 1).astype(jnp.int32)
        blocks = [jnp.take(operand, token_ids, axis=0) for operand in operands]
        if len(blocks) == 1:
            outputs = kernel(blocks[0], w_gate, w_up, w_down)
        else:
            outputs = kernel(blocks[0], blocks[1], w_gate, w_up, w_down)
        return (taken_ids, outputs)
    expert_ids = jnp.arange(N_EXPERT, dtype=jnp.int32)
    taken_all, outputs_all = lax.map(one_expert, (expert_ids, weights[0], weights[1], weights[2]))
    assigned = jnp.zeros((assign_count + 1, D), jnp.bfloat16)
    assigned = assigned.at[taken_all.reshape(-1)].set(outputs_all.reshape(-1, D))
    assigned = assigned[:assign_count].reshape(TOKENS, TOP, D)
    return jnp.einsum('tk,tkd->td', gates, assigned.astype(jnp.float32))

def layer_forward(inputs, gain_row, weights, route, codes):
    widened, scaling, normed = normalize(inputs, gain_row)
    summed = expert_sums(route, gate_values(codes), (normed,), weights, expert_forward)
    return (widened + summed).astype(jnp.bfloat16)

def layer_backward(inputs, upstream, gain_row, weights, route, codes):
    widened, scaling, normed = normalize(inputs, gain_row)
    summed = expert_sums(route, gate_values(codes), (normed, upstream), weights, expert_backward)
    scaled = summed * gain_row
    inner_mean = lax.optimization_barrier(jnp.mean(scaled * widened, axis=-1, keepdims=True))
    cubed = scaling * scaling * scaling
    return (upstream.astype(jnp.float32) + scaling * scaled - widened * cubed * inner_mean).astype(jnp.bfloat16)

def reference(boundary, saved, norm_gain, gate_weight, up_weight, down_weight, routes, gate_codes):
    first_weights = (gate_weight[0], up_weight[0], down_weight[0])
    second_weights = (gate_weight[1], up_weight[1], down_weight[1])
    hidden = layer_forward(boundary[0], norm_gain[0], first_weights, routes[0, 0], gate_codes[0, 0])
    grad_mid = layer_backward(saved[1], boundary[1], norm_gain[1], second_weights, routes[1, 1], gate_codes[1, 1])
    first_out = layer_backward(saved[0], grad_mid, norm_gain[0], first_weights, routes[0, 1], gate_codes[0, 1])
    second_out = layer_forward(hidden, norm_gain[1], second_weights, routes[1, 0], gate_codes[1, 0])
    return jnp.stack([first_out, second_out])
```

```python
import jax
import jax.numpy as jnp
from jax import lax
from jax.sharding import Mesh
from jax.sharding import PartitionSpec as P

EXPERT = ("expert_0", "expert_1", "expert_2", "expert_3")
PLANE = ("expert_0", "expert_1", "expert_3")
RING = "expert_2"

CHUNKS = ((0, -1, 1, -2), (2, -3, 3, 4))
CAPACITY = 6

epsilon = 1e-06


def step_ring(block, step):
    count = lax.axis_size(RING)
    return lax.ppermute(block, RING, [(i, (i + step) % count) for i in range(count)])


def gather_ring(own):
    half = own.shape[0] // 2
    blocks = {0: own}
    for distance in (1, 2, 3):
        blocks[-distance] = step_ring(blocks[1 - distance], 1)
        blocks[distance] = step_ring(blocks[distance - 1], -1)
    blocks[4] = jnp.concatenate(
        (step_ring(blocks[-3][:half], 1), step_ring(blocks[3][half:], -1)), axis=0
    )
    return blocks


def sum_ring(parts):
    half = parts[4].shape[0] // 2
    up = step_ring(parts[4][:half].astype(jnp.bfloat16), 1).astype(jnp.float32)
    down = step_ring(parts[4][half:].astype(jnp.bfloat16), -1).astype(jnp.float32)
    up = jnp.concatenate((parts[3][:half] + up, parts[3][half:]), axis=0)
    down = jnp.concatenate((parts[-3][:half], parts[-3][half:] + down), axis=0)
    for distance in (2, 1):
        up = parts[distance] + step_ring(up.astype(jnp.bfloat16), 1).astype(jnp.float32)
        down = parts[-distance] + step_ring(down.astype(jnp.bfloat16), -1).astype(jnp.float32)
    up = step_ring(up.astype(jnp.bfloat16), 1).astype(jnp.float32)
    down = step_ring(down.astype(jnp.bfloat16), -1).astype(jnp.float32)
    return parts[0] + up + down


def exchange(rows):
    count = lax.axis_size(PLANE)
    parts = rows.reshape(count, -1, rows.shape[-1])
    moved = lax.all_to_all(parts, PLANE, split_axis=0, concat_axis=0, tiled=True)
    return moved.reshape(rows.shape)


def slots(ids, codes):
    width = ids.shape[1]
    tokens = 64
    blocks = width // tokens
    peers = lax.axis_size(PLANE)
    plane = lax.broadcasted_iota(jnp.int32, (peers, 1, 1), 0)
    named = ((plane // 2) * lax.axis_size(RING) + lax.axis_index(RING)) * 2 + plane % 2
    hit = ids[None] == named.astype(jnp.float32)
    member = jnp.sum(hit.astype(jnp.float32), axis=1)
    code = jnp.sum(jnp.where(hit, codes[None], 0.0), axis=1)
    row = lax.broadcasted_iota(jnp.int32, (width, width), 0)
    column = lax.broadcasted_iota(jnp.int32, (width, width), 1)
    earlier = ((row // tokens == column // tokens) & (row < column)).astype(jnp.bfloat16)
    rank = jnp.dot(member.astype(jnp.bfloat16), earlier, preferred_element_type=jnp.float32)
    block = lax.broadcasted_iota(jnp.int32, (1, width), 1) // tokens
    key = jnp.where(member > 0.0, (block * CAPACITY).astype(jnp.float32) + rank, -1.0)
    place = lax.broadcasted_iota(jnp.int32, (1, blocks * CAPACITY, 1), 1).astype(jnp.float32)
    found = key[:, None, :] == place
    picking = found.astype(jnp.bfloat16)
    weighing = jnp.where(found, code[:, None, :], 0.0).astype(jnp.bfloat16)
    return (picking.reshape(-1, width), weighing.reshape(-1, width))


def pick(picking, tokens):
    return jnp.dot(picking, tokens, preferred_element_type=jnp.float32).astype(jnp.bfloat16)


def combine(weighing, rows):
    return lax.dot_general(
        weighing, rows, (((0,), (0,)), ((), ())), preferred_element_type=jnp.float32
    )


def normalize(inputs, gain_row):
    widened = inputs.astype(jnp.float32)
    scaling = lax.rsqrt(jnp.mean(widened * widened, axis=-1, keepdims=True) + epsilon)
    return (widened, scaling, (widened * scaling * gain_row).astype(jnp.bfloat16))


def transposed(left, right):
    return lax.dot_general(
        left, right, (((1,), (1,)), ((), ())), preferred_element_type=jnp.float32
    )


def expert_forward(row_block, w_gate, w_up, w_down):
    gate_part = jnp.dot(row_block, w_gate, preferred_element_type=jnp.float32)
    up_part = jnp.dot(row_block, w_up, preferred_element_type=jnp.float32)
    hidden = (gate_part * jax.nn.sigmoid(gate_part) * up_part).astype(jnp.bfloat16)
    return jnp.dot(hidden, w_down, preferred_element_type=jnp.float32).astype(jnp.bfloat16)


def expert_backward(row_block, grad_block, w_gate, w_up, w_down):
    gate_part = jnp.dot(row_block, w_gate, preferred_element_type=jnp.float32)
    up_part = jnp.dot(row_block, w_up, preferred_element_type=jnp.float32)
    sigmoid_part = jax.nn.sigmoid(gate_part)
    activated = gate_part * sigmoid_part
    slope = sigmoid_part * (1.0 + gate_part * (1.0 - sigmoid_part))
    hidden_grad = transposed(grad_block, w_down)
    gate_grad = (hidden_grad * up_part * slope).astype(jnp.bfloat16)
    up_grad = (hidden_grad * activated).astype(jnp.bfloat16)
    return (transposed(gate_grad, w_gate) + transposed(up_grad, w_up)).astype(jnp.bfloat16)


def apply_expert(forward_flag, rows, grads, weights):
    return lax.cond(
        forward_flag,
        lambda: expert_forward(rows, *weights),
        lambda: expert_backward(rows, grads, *weights),
    )


def finish(widened, scaling, gain_row, upstream, summed, forward_flag):
    forward_out = widened + summed
    scaled = summed * gain_row
    inner_mean = jnp.mean(scaled * widened, axis=-1, keepdims=True)
    cubed = scaling * scaling * scaling
    backward_out = upstream.astype(jnp.float32) + scaling * scaled - widened * cubed * inner_mean
    return jnp.where(forward_flag, forward_out, backward_out).astype(jnp.bfloat16)


def stack(blocks, chunk):
    return jnp.concatenate([blocks[k] for k in chunk], axis=0)


def returned(outcomes, weighings, code_sum):
    parts = {}
    for chunk, outcome, weighing in reversed(list(zip(CHUNKS, outcomes, weighings))):
        share = combine(weighing, exchange(outcome)).reshape(len(chunk), -1, outcome.shape[-1])
        for i, k in enumerate(chunk):
            parts[k] = share[i]
    return sum_ring(parts) / code_sum


def body(boundary, saved, norm_gain, gate_weight, up_weight, down_weight, routes, gate_codes):
    first_segment = lax.axis_index("segment") == 0
    later_forward = jnp.logical_not(first_segment)
    width = boundary.shape[2]
    weights = (gate_weight[0, 0], up_weight[0, 0], down_weight[0, 0])
    gain_row = norm_gain[0]
    edge_rows = boundary[0]
    stored = saved[0]
    route_now = jnp.where(first_segment, routes[0, 0], routes[0, 1])
    codes_now = jnp.where(first_segment, gate_codes[0, 0], gate_codes[0, 1])
    route_next = jnp.where(first_segment, routes[0, 1], routes[0, 0])
    codes_next = jnp.where(first_segment, gate_codes[0, 1], gate_codes[0, 0])
    sum_now = jnp.sum(codes_now.astype(jnp.float32), axis=-1, keepdims=True)
    sum_next = jnp.sum(codes_next.astype(jnp.float32), axis=-1, keepdims=True)
    top = route_now.shape[1]
    info = jnp.concatenate((route_now, codes_now, route_next, codes_next), axis=1)
    info = jnp.pad(info.astype(jnp.bfloat16), ((0, 0), (0, 128 - 4 * top)))

    inputs_now = jnp.where(first_segment, edge_rows, stored)
    widened, scaling, normed = normalize(inputs_now, gain_row)
    stored_normed = normalize(stored, gain_row)[2]
    early_rows = jnp.where(first_segment, stored_normed, edge_rows)

    blocks = gather_ring(jnp.concatenate((normed, info), axis=1))
    early_blocks = gather_ring(early_rows)
    arrived_rows, kept_rows, place_next, weigh_now, weigh_next = [], [], [], [], []
    for chunk in CHUNKS:
        tokens = stack(blocks, chunk)
        told = jnp.transpose(tokens[:, width : width + 4 * top]).astype(jnp.float32)
        pick_now, by_now = slots(told[:top], told[top : 2 * top])
        pick_next, by_next = slots(told[2 * top : 3 * top], told[3 * top :])
        pick_early = jnp.where(first_segment, pick_next, pick_now)
        arrived_rows.append(exchange(pick(pick_now, tokens[:, :width])))
        kept_rows.append(exchange(pick(pick_early, stack(early_blocks, chunk))))
        place_next.append(pick_next)
        weigh_now.append(by_now)
        weigh_next.append(by_next)
    outcomes = [
        apply_expert(first_segment, rows, grads, weights)
        for rows, grads in zip(arrived_rows, kept_rows)
    ]
    summed = returned(outcomes, weigh_now, sum_now)
    produced = finish(widened, scaling, gain_row, edge_rows, summed, first_segment)

    arrived = lax.ppermute(produced, "segment", [(0, 1), (1, 0)])
    inputs_next = jnp.where(first_segment, stored, arrived)
    widened_next, scaling_next, normed_next = normalize(inputs_next, gain_row)
    member_blocks = gather_ring(jnp.where(first_segment, arrived, normed_next))
    outcomes = []
    for i, chunk in enumerate(CHUNKS):
        landed = exchange(pick(place_next[i], stack(member_blocks, chunk)))
        rows = jnp.where(first_segment, kept_rows[i], landed)
        outcomes.append(apply_expert(later_forward, rows, landed, weights))
    summed = returned(outcomes, weigh_next, sum_next)
    result = finish(widened_next, scaling_next, gain_row, arrived, summed, later_forward)
    return result[None]


def solution(mesh):
    finer = Mesh(
        mesh.devices.reshape(mesh.shape["segment"], 4, 2, 8, 2),
        ("segment", "expert_0", "expert_1", "expert_2", "expert_3"),
    )
    placed = (
        P("segment", EXPERT, None),
        P("segment", EXPERT, None),
        P("segment", None),
        P("segment", EXPERT, None, None),
        P("segment", EXPERT, None, None),
        P("segment", EXPERT, None, None),
        P("segment", None, EXPERT, None),
        P("segment", None, EXPERT, None),
    )
    return jax.shard_map(
        body, mesh=finer, in_specs=placed, out_specs=P("segment", EXPERT, None), check_vma=False
    )
```

```python
import functools

import jax
import jax.numpy as jnp
from jax import lax
from jax.experimental import pallas as pl
from jax.experimental.pallas import tpu as pltpu
from jax.sharding import Mesh
from jax.sharding import PartitionSpec as P

EXPERT = ("expert_0", "expert_1", "expert_2", "expert_3")
PLANE = ("expert_0", "expert_1", "expert_3")
RING = "expert_2"

CHUNKS = ((0, -1, 1, -2), (2, -3, 3, 4))
CAPACITY = 6

epsilon = 1e-06


def step_ring(block, step):
    count = lax.axis_size(RING)
    return lax.ppermute(block, RING, [(i, (i + step) % count) for i in range(count)])


def gather_near(own):
    blocks = {0: own}
    for distance in (1, 2):
        blocks[-distance] = step_ring(blocks[1 - distance], 1)
        blocks[distance] = step_ring(blocks[distance - 1], -1)
    return blocks


def gather_far(blocks):
    half = blocks[0].shape[0] // 2
    up, down = step_ring(blocks[-2], 1), step_ring(blocks[2], -1)
    last = jnp.concatenate((step_ring(up[:half], 1), step_ring(down[half:], -1)), axis=0)
    return {**blocks, -3: up, 3: down, 4: last}


def sum_ring(parts):
    half = parts[4].shape[0] // 2
    up = step_ring(parts[4][:half].astype(jnp.bfloat16), 1).astype(jnp.float32)
    down = step_ring(parts[4][half:].astype(jnp.bfloat16), -1).astype(jnp.float32)
    up = jnp.concatenate((parts[3][:half] + up, parts[3][half:]), axis=0)
    down = jnp.concatenate((parts[-3][:half], parts[-3][half:] + down), axis=0)
    for distance in (2, 1):
        up = parts[distance] + step_ring(up.astype(jnp.bfloat16), 1).astype(jnp.float32)
        down = parts[-distance] + step_ring(down.astype(jnp.bfloat16), -1).astype(jnp.float32)
    up = step_ring(up.astype(jnp.bfloat16), 1).astype(jnp.float32)
    down = step_ring(down.astype(jnp.bfloat16), -1).astype(jnp.float32)
    return parts[0] + up + down


def exchange(rows):
    count = lax.axis_size(PLANE)
    parts = rows.reshape(count, -1, rows.shape[-1])
    moved = lax.all_to_all(parts, PLANE, split_axis=0, concat_axis=0, tiled=True)
    return moved.reshape(rows.shape)


def slots(ids, codes):
    width = ids.shape[1]
    tokens = 64
    blocks = width // tokens
    peers = lax.axis_size(PLANE)
    plane = lax.broadcasted_iota(jnp.int32, (peers, 1, 1), 0)
    named = ((plane // 2) * lax.axis_size(RING) + lax.axis_index(RING)) * 2 + plane % 2
    hit = ids[None] == named.astype(jnp.float32)
    member = jnp.sum(hit.astype(jnp.float32), axis=1)
    code = jnp.sum(jnp.where(hit, codes[None], 0.0), axis=1)
    row = lax.broadcasted_iota(jnp.int32, (width, width), 0)
    column = lax.broadcasted_iota(jnp.int32, (width, width), 1)
    earlier = ((row // tokens == column // tokens) & (row < column)).astype(jnp.bfloat16)
    rank = jnp.dot(member.astype(jnp.bfloat16), earlier, preferred_element_type=jnp.float32)
    block = lax.broadcasted_iota(jnp.int32, (1, width), 1) // tokens
    key = jnp.where(member > 0.0, (block * CAPACITY).astype(jnp.float32) + rank, -1.0)
    place = lax.broadcasted_iota(jnp.int32, (1, blocks * CAPACITY, 1), 1).astype(jnp.float32)
    found = key[:, None, :] == place
    picking = found.astype(jnp.bfloat16)
    weighing = jnp.where(found, code[:, None, :], 0.0).astype(jnp.bfloat16)
    return (picking.reshape(-1, width), weighing.reshape(-1, width))


def pick(picking, tokens):
    return jnp.dot(picking, tokens, preferred_element_type=jnp.float32).astype(jnp.bfloat16)


def combine(weighing, rows):
    return lax.dot_general(
        weighing, rows, (((0,), (0,)), ((), ())), preferred_element_type=jnp.float32
    )


def normalize(inputs, gain_row):
    widened = inputs.astype(jnp.float32)
    scaling = lax.rsqrt(jnp.mean(widened * widened, axis=-1, keepdims=True) + epsilon)
    return (widened, scaling, (widened * scaling * gain_row).astype(jnp.bfloat16))


def transposed(left, right):
    return lax.dot_general(
        left, right, (((1,), (1,)), ((), ())), preferred_element_type=jnp.float32
    )


def expert_kernel(forward_from, flag, first, second, w_gate, w_up, w_down, out, total):
    step = pl.program_id(0)
    forward = flag[0] == 1

    @pl.when(step == 0)
    def _():
        total[...] = jnp.zeros_like(total)

    @pl.when(forward)
    def _():
        rows = (first, second)[forward_from][...]
        gate_part = jnp.dot(rows, w_gate[...], preferred_element_type=jnp.float32)
        up_part = jnp.dot(rows, w_up[...], preferred_element_type=jnp.float32)
        hidden = (gate_part * jax.nn.sigmoid(gate_part) * up_part).astype(jnp.bfloat16)
        total[...] += jnp.dot(hidden, w_down[...], preferred_element_type=jnp.float32)

    @pl.when(jnp.logical_not(forward))
    def _():
        rows = first[...]
        gate_part = jnp.dot(rows, w_gate[...], preferred_element_type=jnp.float32)
        up_part = jnp.dot(rows, w_up[...], preferred_element_type=jnp.float32)
        hidden_grad = transposed(second[...], w_down[...])
        sigmoid_part = jax.nn.sigmoid(gate_part)
        activated = gate_part * sigmoid_part
        slope = sigmoid_part * (1.0 + gate_part * (1.0 - sigmoid_part))
        gate_grad = (hidden_grad * up_part * slope).astype(jnp.bfloat16)
        up_grad = (hidden_grad * activated).astype(jnp.bfloat16)
        total[...] += transposed(gate_grad, w_gate[...]) + transposed(up_grad, w_up[...])

    @pl.when(step == pl.num_programs(0) - 1)
    def _():
        out[...] = total[...].astype(jnp.bfloat16)


def apply_expert(flag, first, first_at, second, second_at, forward_from, weights):
    rows, width = first.shape[0], weights[0].shape[0]
    inner = weights[0].shape[1]
    depth = inner // 3
    return pl.pallas_call(
        functools.partial(expert_kernel, forward_from),
        grid=(inner // depth,),
        in_specs=[
            pl.BlockSpec(memory_space=pltpu.SMEM),
            pl.BlockSpec((rows, width), lambda j: (0, first_at)),
            pl.BlockSpec((rows, width), lambda j: (0, second_at)),
            pl.BlockSpec((width, depth), lambda j: (0, j)),
            pl.BlockSpec((width, depth), lambda j: (0, j)),
            pl.BlockSpec((depth, width), lambda j: (j, 0)),
        ],
        out_specs=pl.BlockSpec((rows, width), lambda j: (0, 0)),
        out_shape=jax.ShapeDtypeStruct((rows, width), jnp.bfloat16),
        scratch_shapes=[pltpu.VMEM((rows, width), jnp.float32)],
        cost_estimate=pl.CostEstimate(
            flops=10 * rows * width * inner,
            bytes_accessed=6 * width * (rows + inner),
            transcendentals=rows * inner,
        ),
        compiler_params=pltpu.CompilerParams(vmem_limit_bytes=48 * 1024 * 1024),
    )(flag, first, second, *weights)


def finish(widened, scaling, gain_row, upstream, summed, forward_flag):
    forward_out = widened + summed
    scaled = summed * gain_row
    inner_mean = jnp.mean(scaled * widened, axis=-1, keepdims=True)
    cubed = scaling * scaling * scaling
    backward_out = upstream.astype(jnp.float32) + scaling * scaled - widened * cubed * inner_mean
    return jnp.where(forward_flag, forward_out, backward_out).astype(jnp.bfloat16)


def stack(blocks, chunk):
    return jnp.concatenate([blocks[k] for k in chunk], axis=0)


def after(first, then):
    return lax.optimization_barrier((first, then))


def returned(outcomes, weighings, code_sum):
    near, far = outcomes
    far_back = exchange(far)
    far_back, near = after(far_back, near)
    near_back = exchange(near)
    parts = {}
    for chunk, back, weighing in zip(CHUNKS, (near_back, far_back), weighings):
        share = combine(weighing, back).reshape(len(chunk), -1, back.shape[-1])
        for i, k in enumerate(chunk):
            parts[k] = share[i]
    return sum_ring(parts) / code_sum


def body(boundary, saved, norm_gain, gate_weight, up_weight, down_weight, routes, gate_codes):
    first_segment = lax.axis_index("segment") == 0
    later_forward = jnp.logical_not(first_segment)
    width = boundary.shape[2]
    weights = (gate_weight[0, 0], up_weight[0, 0], down_weight[0, 0])
    gain_row = norm_gain[0]
    edge_rows = boundary[0]
    stored = saved[0]
    route_now = jnp.where(first_segment, routes[0, 0], routes[0, 1])
    codes_now = jnp.where(first_segment, gate_codes[0, 0], gate_codes[0, 1])
    route_next = jnp.where(first_segment, routes[0, 1], routes[0, 0])
    codes_next = jnp.where(first_segment, gate_codes[0, 1], gate_codes[0, 0])
    sum_now = jnp.sum(codes_now.astype(jnp.float32), axis=-1, keepdims=True)
    sum_next = jnp.sum(codes_next.astype(jnp.float32), axis=-1, keepdims=True)
    top = route_now.shape[1]
    info = jnp.concatenate((route_now, codes_now, route_next, codes_next), axis=1)
    info = jnp.pad(info.astype(jnp.bfloat16), ((0, 0), (0, 128 - 4 * top)))

    inputs_now = jnp.where(first_segment, edge_rows, stored)
    widened, scaling, normed = normalize(inputs_now, gain_row)
    stored_normed = normalize(stored, gain_row)[2]
    early_rows = jnp.where(first_segment, stored_normed, edge_rows)

    forward_first = first_segment.astype(jnp.int32).reshape(1)

    blocks = gather_near(jnp.concatenate((normed, early_rows, info), axis=1))
    pairs, place_next, weigh_now, weigh_next = [], [], [], []
    for chunk in CHUNKS:
        if pairs:
            blocks = gather_far(blocks)
        tokens = stack(blocks, chunk)
        told = jnp.transpose(tokens[:, 2 * width : 2 * width + 4 * top]).astype(jnp.float32)
        pick_now, by_now = slots(told[:top], told[top : 2 * top])
        pick_next, by_next = slots(told[2 * top : 3 * top], told[3 * top :])
        pick_early = jnp.where(first_segment, pick_next, pick_now)
        picked = jnp.concatenate(
            (
                pick(pick_now, tokens[:, :width]),
                pick(pick_early, tokens[:, width : 2 * width]),
            ),
            axis=1,
        )
        if pairs:
            pairs[-1], picked = after(pairs[-1], picked)
        else:
            picked, blocks = after(picked, blocks)
        pairs.append(exchange(picked))
        place_next.append(pick_next)
        weigh_now.append(by_now)
        weigh_next.append(by_next)
    outcomes = [apply_expert(forward_first, pair, 0, pair, 1, 0, weights) for pair in pairs]
    summed = returned(outcomes, weigh_now, sum_now)
    produced = finish(widened, scaling, gain_row, edge_rows, summed, first_segment)

    arrived = lax.ppermute(produced, "segment", [(0, 1), (1, 0)])
    inputs_next = jnp.where(first_segment, stored, arrived)
    widened_next, scaling_next, normed_next = normalize(inputs_next, gain_row)
    member_blocks = gather_far(gather_near(jnp.where(first_segment, arrived, normed_next)))
    landed = []
    for i, chunk in enumerate(CHUNKS):
        picked = pick(place_next[i], stack(member_blocks, chunk))
        if landed:
            landed[-1], picked = after(landed[-1], picked)
        landed.append(exchange(picked))
    outcomes = [
        apply_expert(1 - forward_first, pair, 1, rows, 0, 1, weights)
        for pair, rows in zip(pairs, landed)
    ]
    summed = returned(outcomes, weigh_next, sum_next)
    result = finish(widened_next, scaling_next, gain_row, arrived, summed, later_forward)
    return result[None]


def solution(mesh):
    finer = Mesh(
        mesh.devices.reshape(mesh.shape["segment"], 4, 2, 8, 2),
        ("segment", "expert_0", "expert_1", "expert_2", "expert_3"),
    )
    placed = (
        P("segment", EXPERT, None),
        P("segment", EXPERT, None),
        P("segment", None),
        P("segment", EXPERT, None, None),
        P("segment", EXPERT, None, None),
        P("segment", EXPERT, None, None),
        P("segment", None, EXPERT, None),
        P("segment", None, EXPERT, None),
    )
    return jax.shard_map(
        body, mesh=finer, in_specs=placed, out_specs=P("segment", EXPERT, None), check_vma=False
    )
```

```python
import functools

import jax
import jax.numpy as jnp
from jax import lax
from jax.experimental import pallas as pl
from jax.experimental.pallas import tpu as pltpu
from jax.sharding import Mesh
from jax.sharding import PartitionSpec as P

EXPERT = ("expert_0", "expert_1", "expert_2", "expert_3")
PLANE = ("expert_0", "expert_1", "expert_3")
RING = "expert_2"

CHUNKS = ((0, -1, 1, -2), (2, -3, 3, 4))
CAPACITY = 6

epsilon = 1e-06


def step_ring(block, step):
    count = lax.axis_size(RING)
    return lax.ppermute(block, RING, [(i, (i + step) % count) for i in range(count)])


def gather_near(own):
    blocks = {0: own}
    for distance in (1, 2):
        blocks[-distance] = step_ring(blocks[1 - distance], 1)
        blocks[distance] = step_ring(blocks[distance - 1], -1)
    return blocks


def gather_far(blocks):
    half = blocks[0].shape[0] // 2
    up, down = step_ring(blocks[-2], 1), step_ring(blocks[2], -1)
    last = jnp.concatenate((step_ring(up[:half], 1), step_ring(down[half:], -1)), axis=0)
    return {**blocks, -3: up, 3: down, 4: last}


def sum_ring(parts):
    half = parts[4].shape[0] // 2
    up = step_ring(parts[4][:half].astype(jnp.bfloat16), 1).astype(jnp.float32)
    down = step_ring(parts[4][half:].astype(jnp.bfloat16), -1).astype(jnp.float32)
    up = jnp.concatenate((parts[3][:half] + up, parts[3][half:]), axis=0)
    down = jnp.concatenate((parts[-3][:half], parts[-3][half:] + down), axis=0)
    for distance in (2, 1):
        up = parts[distance] + step_ring(up.astype(jnp.bfloat16), 1).astype(jnp.float32)
        down = parts[-distance] + step_ring(down.astype(jnp.bfloat16), -1).astype(jnp.float32)
    up = step_ring(up.astype(jnp.bfloat16), 1).astype(jnp.float32)
    down = step_ring(down.astype(jnp.bfloat16), -1).astype(jnp.float32)
    return parts[0] + up + down


def exchange(rows):
    count = lax.axis_size(PLANE)
    parts = rows.reshape(count, -1, rows.shape[-1])
    moved = lax.all_to_all(parts, PLANE, split_axis=0, concat_axis=0, tiled=True)
    return moved.reshape(rows.shape)


def slots(ids, codes):
    width = ids.shape[1]
    tokens = 64
    blocks = width // tokens
    peers = lax.axis_size(PLANE)
    plane = lax.broadcasted_iota(jnp.int32, (peers, 1, 1), 0)
    named = ((plane // 2) * lax.axis_size(RING) + lax.axis_index(RING)) * 2 + plane % 2
    hit = ids[None] == named.astype(jnp.float32)
    member = jnp.sum(hit.astype(jnp.float32), axis=1)
    code = jnp.sum(jnp.where(hit, codes[None], 0.0), axis=1)
    row = lax.broadcasted_iota(jnp.int32, (width, width), 0)
    column = lax.broadcasted_iota(jnp.int32, (width, width), 1)
    earlier = ((row // tokens == column // tokens) & (row < column)).astype(jnp.bfloat16)
    rank = jnp.dot(member.astype(jnp.bfloat16), earlier, preferred_element_type=jnp.float32)
    block = lax.broadcasted_iota(jnp.int32, (1, width), 1) // tokens
    key = jnp.where(member > 0.0, (block * CAPACITY).astype(jnp.float32) + rank, -1.0)
    place = lax.broadcasted_iota(jnp.int32, (1, blocks * CAPACITY, 1), 1).astype(jnp.float32)
    found = key[:, None, :] == place
    picking = found.astype(jnp.bfloat16)
    weighing = jnp.where(found, code[:, None, :], 0.0).astype(jnp.bfloat16)
    return (picking.reshape(-1, width), weighing.reshape(-1, width))


def pick(picking, tokens):
    return jnp.dot(picking, tokens, preferred_element_type=jnp.float32).astype(jnp.bfloat16)


def combine(weighing, rows):
    return lax.dot_general(
        weighing, rows, (((0,), (0,)), ((), ())), preferred_element_type=jnp.float32
    )


def normalize(inputs, gain_row):
    widened = inputs.astype(jnp.float32)
    scaling = lax.rsqrt(jnp.mean(widened * widened, axis=-1, keepdims=True) + epsilon)
    return (widened, scaling, (widened * scaling * gain_row).astype(jnp.bfloat16))


def transposed(left, right):
    return lax.dot_general(
        left, right, (((1,), (1,)), ((), ())), preferred_element_type=jnp.float32
    )


def expert_kernel(
    first_at, second_at, forward_from, flag, first, second, w_gate, w_up, w_down, out, *scratch
):
    first_rows, second_rows, gate, up, down, made, done = scratch
    rows, width = first_rows.shape
    into = (
        (first.at[:, pl.ds(first_at * width, width)], first_rows),
        (second.at[:, pl.ds(second_at * width, width)], second_rows),
        (w_gate, gate),
        (w_up, up),
        (w_down, down),
    )
    copies = [
        pltpu.make_async_copy(source, target, done.at[i]) for i, (source, target) in enumerate(into)
    ]
    for copy in copies[:3]:
        copy.start()
    for copy in copies[:3]:
        copy.wait()
    for copy in copies[3:]:
        copy.start()
    forward = flag[0] == 1
    piece = width // 4
    given = [
        pltpu.make_async_copy(made.at[:, part], out.at[:, part], done.at[5 + i])
        for i, part in enumerate(pl.ds(i * piece, piece) for i in range(4))
    ]

    @pl.when(forward)
    def _():
        taken = (first_rows, second_rows)[forward_from][...]
        gate_part = jnp.dot(taken, gate[...], preferred_element_type=jnp.float32)
        copies[3].wait()
        up_part = jnp.dot(taken, up[...], preferred_element_type=jnp.float32)
        hidden = (gate_part * jax.nn.sigmoid(gate_part) * up_part).astype(jnp.bfloat16)
        copies[4].wait()
        for i, copy in enumerate(given):
            part = slice(i * piece, (i + 1) * piece)
            total = jnp.dot(hidden, down[:, part], preferred_element_type=jnp.float32)
            made[:, part] = total.astype(jnp.bfloat16)
            copy.start()

    @pl.when(jnp.logical_not(forward))
    def _():
        taken = first_rows[...]
        gate_part = jnp.dot(taken, gate[...], preferred_element_type=jnp.float32)
        copies[3].wait()
        up_part = jnp.dot(taken, up[...], preferred_element_type=jnp.float32)
        copies[4].wait()
        hidden_grad = transposed(second_rows[...], down[...])
        sigmoid_part = jax.nn.sigmoid(gate_part)
        activated = gate_part * sigmoid_part
        slope = sigmoid_part * (1.0 + gate_part * (1.0 - sigmoid_part))
        gate_grad = (hidden_grad * up_part * slope).astype(jnp.bfloat16)
        up_grad = (hidden_grad * activated).astype(jnp.bfloat16)
        for i, copy in enumerate(given):
            part = slice(i * piece, (i + 1) * piece)
            total = transposed(gate_grad, gate[part, :]) + transposed(up_grad, up[part, :])
            made[:, part] = total.astype(jnp.bfloat16)
            copy.start()

    for copy in given:
        copy.wait()


def apply_expert(flag, first, first_at, second, second_at, forward_from, weights):
    rows, (width, inner) = first.shape[0], weights[0].shape
    weights = [pltpu.with_memory_space_constraint(w, pltpu.HBM) for w in weights]
    return pl.pallas_call(
        functools.partial(expert_kernel, first_at, second_at, forward_from),
        in_specs=[pl.BlockSpec(memory_space=pltpu.SMEM)] + [pl.BlockSpec(memory_space=pl.ANY)] * 5,
        out_specs=pl.BlockSpec(memory_space=pl.ANY),
        out_shape=pltpu.HBM((rows, width), jnp.bfloat16),
        scratch_shapes=[pltpu.VMEM((rows, width), jnp.bfloat16)] * 2
        + [pltpu.VMEM(w.shape, w.dtype) for w in weights]
        + [pltpu.VMEM((rows, width), jnp.bfloat16), pltpu.SemaphoreType.DMA((9,))],
        cost_estimate=pl.CostEstimate(
            flops=10 * rows * width * inner,
            bytes_accessed=6 * width * (rows + inner),
            transcendentals=rows * inner,
        ),
        compiler_params=pltpu.CompilerParams(vmem_limit_bytes=48 * 1024 * 1024),
    )(flag, first, second, *weights)


def finish(widened, scaling, gain_row, upstream, summed, forward_flag):
    forward_out = widened + summed
    scaled = summed * gain_row
    inner_mean = jnp.mean(scaled * widened, axis=-1, keepdims=True)
    cubed = scaling * scaling * scaling
    backward_out = upstream.astype(jnp.float32) + scaling * scaled - widened * cubed * inner_mean
    return jnp.where(forward_flag, forward_out, backward_out).astype(jnp.bfloat16)


def stack(blocks, chunk):
    return jnp.concatenate([blocks[k] for k in chunk], axis=0)


def after(first, then):
    return lax.optimization_barrier((first, then))


def returned(outcomes, weighings, code_sum):
    near, far = outcomes
    far_back = exchange(far)
    far_back, near = after(far_back, near)
    near_back = exchange(near)
    parts = {}
    for chunk, back, weighing in zip(CHUNKS, (near_back, far_back), weighings):
        tokens = weighing.shape[1] // len(chunk)
        for i, k in enumerate(chunk):
            parts[k] = combine(weighing[:, i * tokens : (i + 1) * tokens], back)
    return sum_ring(parts) / code_sum


def body(boundary, saved, norm_gain, gate_weight, up_weight, down_weight, routes, gate_codes):
    first_segment = lax.axis_index("segment") == 0
    later_forward = jnp.logical_not(first_segment)
    width = boundary.shape[2]
    weights = (gate_weight[0, 0], up_weight[0, 0], down_weight[0, 0])
    gain_row = norm_gain[0]
    edge_rows = boundary[0]
    stored = saved[0]
    route_now = jnp.where(first_segment, routes[0, 0], routes[0, 1])
    codes_now = jnp.where(first_segment, gate_codes[0, 0], gate_codes[0, 1])
    route_next = jnp.where(first_segment, routes[0, 1], routes[0, 0])
    codes_next = jnp.where(first_segment, gate_codes[0, 1], gate_codes[0, 0])
    sum_now = jnp.sum(codes_now.astype(jnp.float32), axis=-1, keepdims=True)
    sum_next = jnp.sum(codes_next.astype(jnp.float32), axis=-1, keepdims=True)
    top = route_now.shape[1]
    info = jnp.concatenate((route_now, codes_now, route_next, codes_next), axis=1)
    info = jnp.pad(info.astype(jnp.bfloat16), ((0, 0), (0, 128 - 4 * top)))

    inputs_now = jnp.where(first_segment, edge_rows, stored)
    widened, scaling, normed = normalize(inputs_now, gain_row)
    stored_normed = normalize(stored, gain_row)[2]
    early_rows = jnp.where(first_segment, stored_normed, edge_rows)

    forward_first = first_segment.astype(jnp.int32).reshape(1)

    blocks = gather_near(jnp.concatenate((normed, early_rows, info), axis=1))
    pairs, place_next, weigh_now, weigh_next = [], [], [], []
    for chunk in CHUNKS:
        if pairs:
            blocks = gather_far(blocks)
        tokens = stack(blocks, chunk)
        told = jnp.transpose(tokens[:, 2 * width : 2 * width + 4 * top]).astype(jnp.float32)
        pick_now, by_now = slots(told[:top], told[top : 2 * top])
        pick_next, by_next = slots(told[2 * top : 3 * top], told[3 * top :])
        pick_early = jnp.where(first_segment, pick_next, pick_now)
        picked = jnp.concatenate(
            (
                pick(pick_now, tokens[:, :width]),
                pick(pick_early, tokens[:, width : 2 * width]),
            ),
            axis=1,
        )
        if pairs:
            pairs[-1], picked = after(pairs[-1], picked)
        else:
            picked, blocks = after(picked, blocks)
        pairs.append(exchange(picked))
        place_next.append(pick_next)
        weigh_now.append(by_now)
        weigh_next.append(by_next)
    outcomes = [apply_expert(forward_first, pair, 0, pair, 1, 0, weights) for pair in pairs]
    summed = returned(outcomes, weigh_now, sum_now)
    produced = finish(widened, scaling, gain_row, edge_rows, summed, first_segment)

    arrived = lax.ppermute(produced, "segment", [(0, 1), (1, 0)])
    inputs_next = jnp.where(first_segment, stored, arrived)
    widened_next, scaling_next, normed_next = normalize(inputs_next, gain_row)
    member_blocks = gather_far(gather_near(jnp.where(first_segment, arrived, normed_next)))
    landed = []
    for i, chunk in enumerate(CHUNKS):
        picked = pick(place_next[i], stack(member_blocks, chunk))
        if landed:
            landed[-1], picked = after(landed[-1], picked)
        landed.append(exchange(picked))
    outcomes = [
        apply_expert(1 - forward_first, pair, 1, rows, 0, 1, weights)
        for pair, rows in zip(pairs, landed)
    ]
    summed = returned(outcomes, weigh_next, sum_next)
    result = finish(widened_next, scaling_next, gain_row, arrived, summed, later_forward)
    return result[None]


def solution(mesh):
    finer = Mesh(
        mesh.devices.reshape(mesh.shape["segment"], 4, 2, 8, 2),
        ("segment", "expert_0", "expert_1", "expert_2", "expert_3"),
    )
    placed = (
        P("segment", EXPERT, None),
        P("segment", EXPERT, None),
        P("segment", None),
        P("segment", EXPERT, None, None),
        P("segment", EXPERT, None, None),
        P("segment", EXPERT, None, None),
        P("segment", None, EXPERT, None),
        P("segment", None, EXPERT, None),
    )
    return jax.shard_map(
        body, mesh=finer, in_specs=placed, out_specs=P("segment", EXPERT, None), check_vma=False
    )
```

```python
import functools

import jax
import jax.numpy as jnp
from jax import lax
from jax.experimental import pallas as pl
from jax.experimental.pallas import tpu as pltpu
from jax.sharding import Mesh
from jax.sharding import PartitionSpec as P

EXPERT = ("expert_0", "expert_1", "expert_2", "expert_3")
PLANE = ("expert_0", "expert_1", "expert_3")
RING = "expert_2"

CHUNKS = ((0, -1, 1, -2), (2, -3, 3, 4))
CAPACITY = 6

epsilon = 1e-06


def step_ring(block, step):
    count = lax.axis_size(RING)
    return lax.ppermute(block, RING, [(i, (i + step) % count) for i in range(count)])


def gather_near(own):
    blocks = {0: own}
    for distance in (1, 2):
        blocks[-distance] = step_ring(blocks[1 - distance], 1)
        blocks[distance] = step_ring(blocks[distance - 1], -1)
    return blocks


def gather_far(blocks):
    half = blocks[0].shape[0] // 2
    up, down = step_ring(blocks[-2], 1), step_ring(blocks[2], -1)
    last = jnp.concatenate((step_ring(up[:half], 1), step_ring(down[half:], -1)), axis=0)
    return {**blocks, -3: up, 3: down, 4: last}


def add(part, arrived):
    return (part.astype(jnp.float32) + arrived.astype(jnp.float32)).astype(jnp.bfloat16)


def sum_ring(parts):
    half = parts[4].shape[0] // 2
    up = step_ring(parts[4][:half], 1)
    down = step_ring(parts[4][half:], -1)
    up = jnp.concatenate((add(parts[3][:half], up), parts[3][half:]), axis=0)
    down = jnp.concatenate((parts[-3][:half], add(parts[-3][half:], down)), axis=0)
    for distance in (2, 1):
        up = add(parts[distance], step_ring(up, 1))
        down = add(parts[-distance], step_ring(down, -1))
    up, down = step_ring(up, 1), step_ring(down, -1)
    return sum(part.astype(jnp.float32) for part in (parts[0], up, down))


def exchange(rows):
    count = lax.axis_size(PLANE)
    parts = rows.reshape(count, -1, rows.shape[-1])
    moved = lax.all_to_all(parts, PLANE, split_axis=0, concat_axis=0, tiled=True)
    return moved.reshape(rows.shape)


def slots(ids, codes):
    width = ids.shape[1]
    tokens = 64
    blocks = width // tokens
    peers = lax.axis_size(PLANE)
    plane = lax.broadcasted_iota(jnp.int32, (peers, 1, 1), 0)
    named = ((plane // 2) * lax.axis_size(RING) + lax.axis_index(RING)) * 2 + plane % 2
    hit = ids[None] == named.astype(jnp.float32)
    member = jnp.sum(hit.astype(jnp.float32), axis=1)
    code = jnp.sum(jnp.where(hit, codes[None], 0.0), axis=1)
    row = lax.broadcasted_iota(jnp.int32, (width, width), 0)
    column = lax.broadcasted_iota(jnp.int32, (width, width), 1)
    earlier = ((row // tokens == column // tokens) & (row < column)).astype(jnp.bfloat16)
    rank = jnp.dot(member.astype(jnp.bfloat16), earlier, preferred_element_type=jnp.float32)
    block = lax.broadcasted_iota(jnp.int32, (1, width), 1) // tokens
    key = jnp.where(member > 0.0, (block * CAPACITY).astype(jnp.float32) + rank, -1.0)
    place = lax.broadcasted_iota(jnp.int32, (1, blocks * CAPACITY, 1), 1).astype(jnp.float32)
    found = key[:, None, :] == place
    picking = found.astype(jnp.bfloat16)
    weighing = jnp.where(found, code[:, None, :], 0.0).astype(jnp.bfloat16)
    return (picking.reshape(-1, width), weighing.reshape(-1, width))


def pick(picking, tokens):
    return jnp.dot(picking, tokens, preferred_element_type=jnp.float32).astype(jnp.bfloat16)


def combine(weighing, rows):
    return lax.dot_general(
        weighing, rows, (((0,), (0,)), ((), ())), preferred_element_type=jnp.float32
    ).astype(jnp.bfloat16)


def normalize(inputs, gain_row):
    widened = inputs.astype(jnp.float32)
    scaling = lax.rsqrt(jnp.mean(widened * widened, axis=-1, keepdims=True) + epsilon)
    return (widened, scaling, (widened * scaling * gain_row).astype(jnp.bfloat16))


def transposed(left, right):
    return lax.dot_general(
        left, right, (((1,), (1,)), ((), ())), preferred_element_type=jnp.float32
    )


def expert_kernel(
    first_at, second_at, forward_from, flag, first, second, w_gate, w_up, w_down, out, *scratch
):
    first_rows, second_rows, gate, up, down, made, done = scratch
    rows, width = first_rows.shape
    into = (
        (first.at[:, pl.ds(first_at * width, width)], first_rows),
        (second.at[:, pl.ds(second_at * width, width)], second_rows),
        (w_gate, gate),
        (w_up, up),
        (w_down, down),
    )
    copies = [
        pltpu.make_async_copy(source, target, done.at[i]) for i, (source, target) in enumerate(into)
    ]
    for copy in copies[:3]:
        copy.start()
    for copy in copies[:3]:
        copy.wait()
    for copy in copies[3:]:
        copy.start()
    forward = flag[0] == 1
    piece = width // 4
    given = [
        pltpu.make_async_copy(made.at[:, part], out.at[:, part], done.at[5 + i])
        for i, part in enumerate(pl.ds(i * piece, piece) for i in range(4))
    ]

    @pl.when(forward)
    def _():
        taken = (first_rows, second_rows)[forward_from][...]
        gate_part = jnp.dot(taken, gate[...], preferred_element_type=jnp.float32)
        copies[3].wait()
        up_part = jnp.dot(taken, up[...], preferred_element_type=jnp.float32)
        hidden = (gate_part * jax.nn.sigmoid(gate_part) * up_part).astype(jnp.bfloat16)
        copies[4].wait()
        for i, copy in enumerate(given):
            part = slice(i * piece, (i + 1) * piece)
            total = jnp.dot(hidden, down[:, part], preferred_element_type=jnp.float32)
            made[:, part] = total.astype(jnp.bfloat16)
            copy.start()

    @pl.when(jnp.logical_not(forward))
    def _():
        taken = first_rows[...]
        gate_part = jnp.dot(taken, gate[...], preferred_element_type=jnp.float32)
        copies[3].wait()
        up_part = jnp.dot(taken, up[...], preferred_element_type=jnp.float32)
        copies[4].wait()
        hidden_grad = transposed(second_rows[...], down[...])
        sigmoid_part = jax.nn.sigmoid(gate_part)
        activated = gate_part * sigmoid_part
        slope = sigmoid_part * (1.0 + gate_part * (1.0 - sigmoid_part))
        gate_grad = (hidden_grad * up_part * slope).astype(jnp.bfloat16)
        up_grad = (hidden_grad * activated).astype(jnp.bfloat16)
        for i, copy in enumerate(given):
            part = slice(i * piece, (i + 1) * piece)
            total = transposed(gate_grad, gate[part, :]) + transposed(up_grad, up[part, :])
            made[:, part] = total.astype(jnp.bfloat16)
            copy.start()

    for copy in given:
        copy.wait()


def apply_expert(flag, first, first_at, second, second_at, forward_from, weights):
    rows, (width, inner) = first.shape[0], weights[0].shape
    weights = [pltpu.with_memory_space_constraint(w, pltpu.HBM) for w in weights]
    return pl.pallas_call(
        functools.partial(expert_kernel, first_at, second_at, forward_from),
        in_specs=[pl.BlockSpec(memory_space=pltpu.SMEM)] + [pl.BlockSpec(memory_space=pl.ANY)] * 5,
        out_specs=pl.BlockSpec(memory_space=pl.ANY),
        out_shape=pltpu.HBM((rows, width), jnp.bfloat16),
        scratch_shapes=[pltpu.VMEM((rows, width), jnp.bfloat16)] * 2
        + [pltpu.VMEM(w.shape, w.dtype) for w in weights]
        + [pltpu.VMEM((rows, width), jnp.bfloat16), pltpu.SemaphoreType.DMA((9,))],
        cost_estimate=pl.CostEstimate(
            flops=10 * rows * width * inner,
            bytes_accessed=6 * width * (rows + inner),
            transcendentals=rows * inner,
        ),
        compiler_params=pltpu.CompilerParams(vmem_limit_bytes=48 * 1024 * 1024),
    )(flag, first, second, *weights)


def finish(widened, scaling, gain_row, upstream, summed, forward_flag):
    forward_out = widened + summed
    scaled = summed * gain_row
    inner_mean = jnp.mean(scaled * widened, axis=-1, keepdims=True)
    cubed = scaling * scaling * scaling
    backward_out = upstream.astype(jnp.float32) + scaling * scaled - widened * cubed * inner_mean
    return jnp.where(forward_flag, forward_out, backward_out).astype(jnp.bfloat16)


def stack(blocks, chunk):
    return jnp.concatenate([blocks[k] for k in chunk], axis=0)


def after(first, then):
    return lax.optimization_barrier((first, then))


def returned(outcomes, weighings, code_sum):
    near, far = outcomes
    far_back = exchange(far)
    far_back, near = after(far_back, near)
    near_back = exchange(near)
    parts = {}
    for chunk, back, weighing in zip(CHUNKS, (near_back, far_back), weighings):
        share = combine(weighing, back).reshape(len(chunk), -1, back.shape[-1])
        for i, k in enumerate(chunk):
            parts[k] = share[i]
    return sum_ring(parts) / code_sum


def body(boundary, saved, norm_gain, gate_weight, up_weight, down_weight, routes, gate_codes):
    first_segment = lax.axis_index("segment") == 0
    later_forward = jnp.logical_not(first_segment)
    width = boundary.shape[2]
    weights = (gate_weight[0, 0], up_weight[0, 0], down_weight[0, 0])
    gain_row = norm_gain[0]
    edge_rows = boundary[0]
    stored = saved[0]
    route_now = jnp.where(first_segment, routes[0, 0], routes[0, 1])
    codes_now = jnp.where(first_segment, gate_codes[0, 0], gate_codes[0, 1])
    route_next = jnp.where(first_segment, routes[0, 1], routes[0, 0])
    codes_next = jnp.where(first_segment, gate_codes[0, 1], gate_codes[0, 0])
    sum_now = jnp.sum(codes_now.astype(jnp.float32), axis=-1, keepdims=True)
    sum_next = jnp.sum(codes_next.astype(jnp.float32), axis=-1, keepdims=True)
    top = route_now.shape[1]
    info = jnp.concatenate((route_now, codes_now, route_next, codes_next), axis=1)
    info = jnp.pad(info.astype(jnp.bfloat16), ((0, 0), (0, 128 - 4 * top)))

    inputs_now = jnp.where(first_segment, edge_rows, stored)
    widened, scaling, normed = normalize(inputs_now, gain_row)
    stored_normed = normalize(stored, gain_row)[2]
    early_rows = jnp.where(first_segment, stored_normed, edge_rows)

    forward_first = first_segment.astype(jnp.int32).reshape(1)

    blocks = gather_near(jnp.concatenate((normed, early_rows, info), axis=1))
    pairs, place_next, weigh_now, weigh_next = [], [], [], []
    for chunk in CHUNKS:
        if pairs:
            blocks = gather_far(blocks)
        tokens = stack(blocks, chunk)
        told = jnp.transpose(tokens[:, 2 * width : 2 * width + 4 * top]).astype(jnp.float32)
        pick_now, by_now = slots(told[:top], told[top : 2 * top])
        pick_next, by_next = slots(told[2 * top : 3 * top], told[3 * top :])
        pick_early = jnp.where(first_segment, pick_next, pick_now)
        picked = jnp.concatenate(
            (
                pick(pick_now, tokens[:, :width]),
                pick(pick_early, tokens[:, width : 2 * width]),
            ),
            axis=1,
        )
        if pairs:
            pairs[-1], picked = after(pairs[-1], picked)
        else:
            picked, blocks = after(picked, blocks)
        pairs.append(exchange(picked))
        place_next.append(pick_next)
        weigh_now.append(by_now)
        weigh_next.append(by_next)
    outcomes = [apply_expert(forward_first, pair, 0, pair, 1, 0, weights) for pair in pairs]
    summed = returned(outcomes, weigh_now, sum_now)
    produced = finish(widened, scaling, gain_row, edge_rows, summed, first_segment)

    arrived = lax.ppermute(produced, "segment", [(0, 1), (1, 0)])
    inputs_next = jnp.where(first_segment, stored, arrived)
    widened_next, scaling_next, normed_next = normalize(inputs_next, gain_row)
    member_blocks = gather_far(gather_near(jnp.where(first_segment, arrived, normed_next)))
    landed = []
    for i, chunk in enumerate(CHUNKS):
        picked = pick(place_next[i], stack(member_blocks, chunk))
        if landed:
            landed[-1], picked = after(landed[-1], picked)
        landed.append(exchange(picked))
    outcomes = [
        apply_expert(1 - forward_first, pair, 1, rows, 0, 1, weights)
        for pair, rows in zip(pairs, landed)
    ]
    summed = returned(outcomes, weigh_next, sum_next)
    result = finish(widened_next, scaling_next, gain_row, arrived, summed, later_forward)
    return result[None]


def solution(mesh):
    finer = Mesh(
        mesh.devices.reshape(mesh.shape["segment"], 4, 2, 8, 2),
        ("segment", "expert_0", "expert_1", "expert_2", "expert_3"),
    )
    placed = (
        P("segment", EXPERT, None),
        P("segment", EXPERT, None),
        P("segment", None),
        P("segment", EXPERT, None, None),
        P("segment", EXPERT, None, None),
        P("segment", EXPERT, None, None),
        P("segment", None, EXPERT, None),
        P("segment", None, EXPERT, None),
    )
    return jax.shard_map(
        body, mesh=finer, in_specs=placed, out_specs=P("segment", EXPERT, None), check_vma=False
    )
```

```python
import functools

import jax
import jax.numpy as jnp
from jax import lax
from jax.experimental import pallas as pl
from jax.experimental.pallas import tpu as pltpu
from jax.sharding import Mesh
from jax.sharding import PartitionSpec as P

EXPERT = ("expert_0", "expert_1", "expert_2", "expert_3")
PLANE = ("expert_0", "expert_1", "expert_3")
RING = "expert_2"

CHUNKS = ((0, -1, 1, -2), (2, -3, 3, 4))
CAPACITY = 6
TOKENS = 64

epsilon = 1e-06


def step_ring(block, step):
    count = lax.axis_size(RING)
    return lax.ppermute(block, RING, [(i, (i + step) % count) for i in range(count)])


def gather_near(own):
    blocks = {0: own}
    for distance in (1, 2):
        blocks[-distance] = step_ring(blocks[1 - distance], 1)
        blocks[distance] = step_ring(blocks[distance - 1], -1)
    return blocks


def gather_far(blocks):
    half = blocks[0].shape[0] // 2
    up, down = step_ring(blocks[-2], 1), step_ring(blocks[2], -1)
    last = jnp.concatenate((step_ring(up[:half], 1), step_ring(down[half:], -1)), axis=0)
    return {**blocks, -3: up, 3: down, 4: last}


def add(part, arrived):
    return (part.astype(jnp.float32) + arrived.astype(jnp.float32)).astype(jnp.bfloat16)


def sum_ring(parts):
    half = parts[4].shape[0] // 2
    up = step_ring(parts[4][:half], 1)
    down = step_ring(parts[4][half:], -1)
    up = jnp.concatenate((add(parts[3][:half], up), parts[3][half:]), axis=0)
    down = jnp.concatenate((parts[-3][:half], add(parts[-3][half:], down)), axis=0)
    for distance in (2, 1):
        up = add(parts[distance], step_ring(up, 1))
        down = add(parts[-distance], step_ring(down, -1))
    up, down = step_ring(up, 1), step_ring(down, -1)
    return sum(part.astype(jnp.float32) for part in (parts[0], up, down))


def exchange(rows):
    count = lax.axis_size(PLANE)
    parts = rows.reshape(count, -1, rows.shape[-1])
    moved = lax.all_to_all(parts, PLANE, split_axis=0, concat_axis=0, tiled=True)
    return moved.reshape(rows.shape)


def one_hots(ids, codes, first_chip, ring, peers):
    width = ids.shape[1]
    blocks = width // TOKENS
    plane = lax.broadcasted_iota(jnp.int32, (peers, 1), 0)
    named = ((((plane >> 1) * ring + first_chip) << 1) + (plane & 1)).astype(jnp.float32)
    member = jnp.zeros((peers, width), jnp.float32)
    code = jnp.zeros((peers, width), jnp.float32)
    for k in range(ids.shape[0]):
        hit = ids[k : k + 1, :] == named
        member = jnp.where(hit, 1.0, member)
        code = jnp.where(hit, codes[k : k + 1, :], code)
    row = lax.broadcasted_iota(jnp.int32, (width, width), 0)
    column = lax.broadcasted_iota(jnp.int32, (width, width), 1)
    earlier = jnp.where((row // TOKENS == column // TOKENS) & (row < column), 1.0, 0.0)
    rank = jnp.dot(
        member.astype(jnp.bfloat16),
        earlier.astype(jnp.bfloat16),
        preferred_element_type=jnp.float32,
    )
    block = lax.broadcasted_iota(jnp.int32, (1, width), 1) // TOKENS
    key = jnp.where(member > 0.0, (block * CAPACITY).astype(jnp.float32) + rank, -1.0)
    rows = blocks * CAPACITY
    place = lax.broadcasted_iota(jnp.int32, (peers, rows, width), 1).astype(jnp.float32)
    found = jnp.broadcast_to(key[:, None, :], (peers, rows, width)) == place
    picking = jnp.where(found, 1.0, 0.0)
    weighing = jnp.where(found, jnp.broadcast_to(code[:, None, :], (peers, rows, width)), 0.0)
    return (picking.reshape(-1, width), weighing.reshape(-1, width))


def pick_kernel(top, ring, peers, told, *refs):
    count = len(refs) - 5
    blocks, (picked, next_out, by_now_out, by_next_out, held) = refs[:count], refs[count:]
    width = picked.shape[1] // 2
    for i, block in enumerate(blocks):
        held[i * TOKENS : (i + 1) * TOKENS, :] = block[...]
    info = jnp.transpose(held[:, 2 * width :].astype(jnp.float32))
    ids_now, codes_now, ids_next, codes_next = (info[i * top : (i + 1) * top, :] for i in range(4))
    pick_now, by_now = one_hots(ids_now, codes_now, told[0], ring, peers)
    pick_next, by_next = one_hots(ids_next, codes_next, told[0], ring, peers)
    early = jnp.where(told[1] == 1, pick_next, pick_now).astype(jnp.bfloat16)
    pick_now = pick_now.astype(jnp.bfloat16)
    picked[:, :width] = jnp.dot(
        pick_now, held[:, :width], preferred_element_type=jnp.float32
    ).astype(jnp.bfloat16)
    picked[:, width:] = jnp.dot(
        early, held[:, width : 2 * width], preferred_element_type=jnp.float32
    ).astype(jnp.bfloat16)
    next_out[...] = pick_next.astype(jnp.bfloat16)
    by_now_out[...] = by_now.astype(jnp.bfloat16)
    by_next_out[...] = by_next.astype(jnp.bfloat16)


def pick_both(told, blocks, top, width):
    ring, peers = lax.axis_size(RING), lax.axis_size(PLANE)
    tokens = len(blocks) * TOKENS
    rows = peers * len(blocks) * CAPACITY
    whole = pl.BlockSpec(memory_space=pltpu.VMEM)
    kept = pltpu.HBM((rows, tokens), jnp.bfloat16)
    blocks = [pltpu.with_memory_space_constraint(block, pltpu.HBM) for block in blocks]
    return pl.pallas_call(
        functools.partial(pick_kernel, top, ring, peers),
        in_specs=[pl.BlockSpec(memory_space=pltpu.SMEM)] + [whole] * len(blocks),
        out_specs=[whole] * 4,
        out_shape=[pltpu.HBM((rows, 2 * width), jnp.bfloat16), kept, kept, kept],
        scratch_shapes=[pltpu.VMEM((tokens, blocks[0].shape[1]), jnp.bfloat16)],
        cost_estimate=pl.CostEstimate(
            flops=4 * rows * tokens * width,
            bytes_accessed=4 * width * (tokens + rows) + 6 * rows * tokens,
            transcendentals=0,
        ),
        compiler_params=pltpu.CompilerParams(vmem_limit_bytes=32 * 1024 * 1024),
    )(told, *blocks)


def pick(picking, tokens):
    return jnp.dot(picking, tokens, preferred_element_type=jnp.float32).astype(jnp.bfloat16)


def combine(weighing, rows):
    return lax.dot_general(
        weighing, rows, (((0,), (0,)), ((), ())), preferred_element_type=jnp.float32
    ).astype(jnp.bfloat16)


def normalize(inputs, gain_row):
    widened = inputs.astype(jnp.float32)
    scaling = lax.rsqrt(jnp.mean(widened * widened, axis=-1, keepdims=True) + epsilon)
    return (widened, scaling, (widened * scaling * gain_row).astype(jnp.bfloat16))


def transposed(left, right):
    return lax.dot_general(
        left, right, (((1,), (1,)), ((), ())), preferred_element_type=jnp.float32
    )


def expert_kernel(
    first_at, second_at, forward_from, flag, first, second, w_gate, w_up, w_down, out, *scratch
):
    first_rows, second_rows, gate, up, down, made, done = scratch
    rows, width = first_rows.shape
    into = (
        (first.at[:, pl.ds(first_at * width, width)], first_rows),
        (second.at[:, pl.ds(second_at * width, width)], second_rows),
        (w_gate, gate),
        (w_up, up),
        (w_down, down),
    )
    copies = [
        pltpu.make_async_copy(source, target, done.at[i]) for i, (source, target) in enumerate(into)
    ]
    for copy in copies[:3]:
        copy.start()
    for copy in copies[:3]:
        copy.wait()
    for copy in copies[3:]:
        copy.start()
    forward = flag[0] == 1
    piece = width // 4
    given = [
        pltpu.make_async_copy(made.at[:, part], out.at[:, part], done.at[5 + i])
        for i, part in enumerate(pl.ds(i * piece, piece) for i in range(4))
    ]

    @pl.when(forward)
    def _():
        taken = (first_rows, second_rows)[forward_from][...]
        gate_part = jnp.dot(taken, gate[...], preferred_element_type=jnp.float32)
        copies[3].wait()
        up_part = jnp.dot(taken, up[...], preferred_element_type=jnp.float32)
        hidden = (gate_part * jax.nn.sigmoid(gate_part) * up_part).astype(jnp.bfloat16)
        copies[4].wait()
        for i, copy in enumerate(given):
            part = slice(i * piece, (i + 1) * piece)
            total = jnp.dot(hidden, down[:, part], preferred_element_type=jnp.float32)
            made[:, part] = total.astype(jnp.bfloat16)
            copy.start()

    @pl.when(jnp.logical_not(forward))
    def _():
        taken = first_rows[...]
        gate_part = jnp.dot(taken, gate[...], preferred_element_type=jnp.float32)
        copies[3].wait()
        up_part = jnp.dot(taken, up[...], preferred_element_type=jnp.float32)
        copies[4].wait()
        hidden_grad = transposed(second_rows[...], down[...])
        sigmoid_part = jax.nn.sigmoid(gate_part)
        activated = gate_part * sigmoid_part
        slope = sigmoid_part * (1.0 + gate_part * (1.0 - sigmoid_part))
        gate_grad = (hidden_grad * up_part * slope).astype(jnp.bfloat16)
        up_grad = (hidden_grad * activated).astype(jnp.bfloat16)
        for i, copy in enumerate(given):
            part = slice(i * piece, (i + 1) * piece)
            total = transposed(gate_grad, gate[part, :]) + transposed(up_grad, up[part, :])
            made[:, part] = total.astype(jnp.bfloat16)
            copy.start()

    for copy in given:
        copy.wait()


def apply_expert(flag, first, first_at, second, second_at, forward_from, weights):
    rows, (width, inner) = first.shape[0], weights[0].shape
    weights = [pltpu.with_memory_space_constraint(w, pltpu.HBM) for w in weights]
    return pl.pallas_call(
        functools.partial(expert_kernel, first_at, second_at, forward_from),
        in_specs=[pl.BlockSpec(memory_space=pltpu.SMEM)] + [pl.BlockSpec(memory_space=pl.ANY)] * 5,
        out_specs=pl.BlockSpec(memory_space=pl.ANY),
        out_shape=pltpu.HBM((rows, width), jnp.bfloat16),
        scratch_shapes=[pltpu.VMEM((rows, width), jnp.bfloat16)] * 2
        + [pltpu.VMEM(w.shape, w.dtype) for w in weights]
        + [pltpu.VMEM((rows, width), jnp.bfloat16), pltpu.SemaphoreType.DMA((9,))],
        cost_estimate=pl.CostEstimate(
            flops=10 * rows * width * inner,
            bytes_accessed=6 * width * (rows + inner),
            transcendentals=rows * inner,
        ),
        compiler_params=pltpu.CompilerParams(vmem_limit_bytes=48 * 1024 * 1024),
    )(flag, first, second, *weights)


def finish(widened, scaling, gain_row, upstream, summed, forward_flag):
    forward_out = widened + summed
    scaled = summed * gain_row
    inner_mean = jnp.mean(scaled * widened, axis=-1, keepdims=True)
    cubed = scaling * scaling * scaling
    backward_out = upstream.astype(jnp.float32) + scaling * scaled - widened * cubed * inner_mean
    return jnp.where(forward_flag, forward_out, backward_out).astype(jnp.bfloat16)


def stack(blocks, chunk):
    return jnp.concatenate([blocks[k] for k in chunk], axis=0)


def after(first, then):
    return lax.optimization_barrier((first, then))


def returned(outcomes, weighings, code_sum):
    near, far = outcomes
    far_back = exchange(far)
    far_back, near = after(far_back, near)
    near_back = exchange(near)
    parts = {}
    for chunk, back, weighing in zip(CHUNKS, (near_back, far_back), weighings):
        share = combine(weighing, back).reshape(len(chunk), -1, back.shape[-1])
        for i, k in enumerate(chunk):
            parts[k] = share[i]
    return sum_ring(parts) / code_sum


def body(boundary, saved, norm_gain, gate_weight, up_weight, down_weight, routes, gate_codes):
    first_segment = lax.axis_index("segment") == 0
    later_forward = jnp.logical_not(first_segment)
    width = boundary.shape[2]
    weights = (gate_weight[0, 0], up_weight[0, 0], down_weight[0, 0])
    gain_row = norm_gain[0]
    edge_rows = boundary[0]
    stored = saved[0]
    route_now = jnp.where(first_segment, routes[0, 0], routes[0, 1])
    codes_now = jnp.where(first_segment, gate_codes[0, 0], gate_codes[0, 1])
    route_next = jnp.where(first_segment, routes[0, 1], routes[0, 0])
    codes_next = jnp.where(first_segment, gate_codes[0, 1], gate_codes[0, 0])
    sum_now = jnp.sum(codes_now.astype(jnp.float32), axis=-1, keepdims=True)
    sum_next = jnp.sum(codes_next.astype(jnp.float32), axis=-1, keepdims=True)
    top = route_now.shape[1]
    info = jnp.concatenate((route_now, codes_now, route_next, codes_next), axis=1)
    info = jnp.pad(info.astype(jnp.bfloat16), ((0, 0), (0, 128 - 4 * top)))

    inputs_now = jnp.where(first_segment, edge_rows, stored)
    widened, scaling, normed = normalize(inputs_now, gain_row)
    stored_normed = normalize(stored, gain_row)[2]
    early_rows = jnp.where(first_segment, stored_normed, edge_rows)

    forward_first = first_segment.astype(jnp.int32).reshape(1)
    told = jnp.stack((lax.axis_index(RING), first_segment.astype(jnp.int32)))

    blocks = gather_near(jnp.concatenate((normed, early_rows, info), axis=1))
    pairs, place_next, weigh_now, weigh_next = [], [], [], []
    for chunk in CHUNKS:
        if pairs:
            blocks = gather_far(blocks)
        picked, pick_next, by_now, by_next = pick_both(
            told, [blocks[k] for k in chunk], top, width
        )
        if pairs:
            pairs[-1], picked = after(pairs[-1], picked)
        else:
            picked, blocks = after(picked, blocks)
        pairs.append(exchange(picked))
        place_next.append(pick_next)
        weigh_now.append(by_now)
        weigh_next.append(by_next)
    outcomes = [apply_expert(forward_first, pair, 0, pair, 1, 0, weights) for pair in pairs]
    summed = returned(outcomes, weigh_now, sum_now)
    produced = finish(widened, scaling, gain_row, edge_rows, summed, first_segment)

    arrived = lax.ppermute(produced, "segment", [(0, 1), (1, 0)])
    inputs_next = jnp.where(first_segment, stored, arrived)
    widened_next, scaling_next, normed_next = normalize(inputs_next, gain_row)
    member_blocks = gather_far(gather_near(jnp.where(first_segment, arrived, normed_next)))
    landed = []
    for i, chunk in enumerate(CHUNKS):
        picked = pick(place_next[i], stack(member_blocks, chunk))
        if landed:
            landed[-1], picked = after(landed[-1], picked)
        landed.append(exchange(picked))
    outcomes = [
        apply_expert(1 - forward_first, pair, 1, rows, 0, 1, weights)
        for pair, rows in zip(pairs, landed)
    ]
    summed = returned(outcomes, weigh_next, sum_next)
    result = finish(widened_next, scaling_next, gain_row, arrived, summed, later_forward)
    return result[None]


def solution(mesh):
    finer = Mesh(
        mesh.devices.reshape(mesh.shape["segment"], 4, 2, 8, 2),
        ("segment", "expert_0", "expert_1", "expert_2", "expert_3"),
    )
    placed = (
        P("segment", EXPERT, None),
        P("segment", EXPERT, None),
        P("segment", None),
        P("segment", EXPERT, None, None),
        P("segment", EXPERT, None, None),
        P("segment", EXPERT, None, None),
        P("segment", None, EXPERT, None),
        P("segment", None, EXPERT, None),
    )
    return jax.shard_map(
        body, mesh=finer, in_specs=placed, out_specs=P("segment", EXPERT, None), check_vma=False
    )
```

```python
import functools

import jax
import jax.numpy as jnp
from jax import lax
from jax.experimental import pallas as pl
from jax.experimental.pallas import tpu as pltpu
from jax.sharding import Mesh
from jax.sharding import PartitionSpec as P

EXPERT = ("expert_0", "expert_1", "expert_2", "expert_3")
PLANE = ("expert_0", "expert_1", "expert_3")
RING = "expert_2"

CHUNKS = ((0, -1, 1, -2), (2, -3, 3, 4))
CAPACITY = 6
TOKENS = 64

epsilon = 1e-06


def step_ring(block, step):
    count = lax.axis_size(RING)
    return lax.ppermute(block, RING, [(i, (i + step) % count) for i in range(count)])


def gather_near(own):
    blocks = {0: own}
    for distance in (1, 2):
        blocks[-distance] = step_ring(blocks[1 - distance], 1)
        blocks[distance] = step_ring(blocks[distance - 1], -1)
    return blocks


def gather_far(blocks):
    half = blocks[0].shape[0] // 2
    up, down = step_ring(blocks[-2], 1), step_ring(blocks[2], -1)
    last = jnp.concatenate((step_ring(up[:half], 1), step_ring(down[half:], -1)), axis=0)
    return {**blocks, -3: up, 3: down, 4: last}


def add(part, arrived):
    return (part.astype(jnp.float32) + arrived.astype(jnp.float32)).astype(jnp.bfloat16)


def sum_ring(parts):
    first, last = parts[4]
    half = first.shape[0]
    up, down = step_ring(first, 1), step_ring(last, -1)
    up = jnp.concatenate((add(parts[3][:half], up), parts[3][half:]), axis=0)
    down = jnp.concatenate((parts[-3][:half], add(parts[-3][half:], down)), axis=0)
    for distance in (2, 1):
        up = add(parts[distance], step_ring(up, 1))
        down = add(parts[-distance], step_ring(down, -1))
    up, down = step_ring(up, 1), step_ring(down, -1)
    return sum(part.astype(jnp.float32) for part in (parts[0], up, down))


def exchange(rows):
    count = lax.axis_size(PLANE)
    parts = rows.reshape(count, -1, rows.shape[-1])
    moved = lax.all_to_all(parts, PLANE, split_axis=0, concat_axis=0, tiled=True)
    return moved.reshape(rows.shape)


def one_hots(ids, codes, first_chip, ring, peers):
    width = ids.shape[1]
    blocks = width // TOKENS
    plane = lax.broadcasted_iota(jnp.int32, (peers, 1), 0)
    named = ((((plane >> 1) * ring + first_chip) << 1) + (plane & 1)).astype(jnp.float32)
    member = jnp.zeros((peers, width), jnp.float32)
    code = jnp.zeros((peers, width), jnp.float32)
    for k in range(ids.shape[0]):
        hit = ids[k : k + 1, :] == named
        member = jnp.where(hit, 1.0, member)
        code = jnp.where(hit, codes[k : k + 1, :], code)
    row = lax.broadcasted_iota(jnp.int32, (width, width), 0)
    column = lax.broadcasted_iota(jnp.int32, (width, width), 1)
    earlier = jnp.where((row // TOKENS == column // TOKENS) & (row < column), 1.0, 0.0)
    rank = jnp.dot(
        member.astype(jnp.bfloat16),
        earlier.astype(jnp.bfloat16),
        preferred_element_type=jnp.float32,
    )
    block = lax.broadcasted_iota(jnp.int32, (1, width), 1) // TOKENS
    key = jnp.where(member > 0.0, (block * CAPACITY).astype(jnp.float32) + rank, -1.0)
    rows = blocks * CAPACITY
    place = lax.broadcasted_iota(jnp.int32, (peers, rows, width), 1).astype(jnp.float32)
    found = jnp.broadcast_to(key[:, None, :], (peers, rows, width)) == place
    picking = jnp.where(found, 1.0, 0.0)
    weighing = jnp.where(found, jnp.broadcast_to(code[:, None, :], (peers, rows, width)), 0.0)
    return (picking.reshape(-1, width), weighing.reshape(-1, width))


def pick_kernel(top, ring, peers, told, *refs):
    count = len(refs) - 5
    blocks, (picked, next_out, by_now_out, by_next_out, held) = refs[:count], refs[count:]
    width = picked.shape[1] // 2
    for i, block in enumerate(blocks):
        held[i * TOKENS : (i + 1) * TOKENS, :] = block[...]
    info = jnp.transpose(held[:, 2 * width :].astype(jnp.float32))
    ids_now, codes_now, ids_next, codes_next = (info[i * top : (i + 1) * top, :] for i in range(4))
    pick_now, by_now = one_hots(ids_now, codes_now, told[0], ring, peers)
    pick_next, by_next = one_hots(ids_next, codes_next, told[0], ring, peers)
    early = jnp.where(told[1] == 1, pick_next, pick_now).astype(jnp.bfloat16)
    pick_now = pick_now.astype(jnp.bfloat16)
    picked[:, :width] = jnp.dot(
        pick_now, held[:, :width], preferred_element_type=jnp.float32
    ).astype(jnp.bfloat16)
    picked[:, width:] = jnp.dot(
        early, held[:, width : 2 * width], preferred_element_type=jnp.float32
    ).astype(jnp.bfloat16)
    next_out[...] = pick_next.astype(jnp.bfloat16)
    by_now_out[...] = by_now.astype(jnp.bfloat16)
    by_next_out[...] = by_next.astype(jnp.bfloat16)


def pick_both(told, blocks, top, width):
    ring, peers = lax.axis_size(RING), lax.axis_size(PLANE)
    tokens = len(blocks) * TOKENS
    rows = peers * len(blocks) * CAPACITY
    whole = pl.BlockSpec(memory_space=pltpu.VMEM)
    kept = pltpu.HBM((rows, tokens), jnp.bfloat16)
    blocks = [pltpu.with_memory_space_constraint(block, pltpu.HBM) for block in blocks]
    return pl.pallas_call(
        functools.partial(pick_kernel, top, ring, peers),
        in_specs=[pl.BlockSpec(memory_space=pltpu.SMEM)] + [whole] * len(blocks),
        out_specs=[whole] * 4,
        out_shape=[pltpu.HBM((rows, 2 * width), jnp.bfloat16), kept, kept, kept],
        scratch_shapes=[pltpu.VMEM((tokens, blocks[0].shape[1]), jnp.bfloat16)],
        cost_estimate=pl.CostEstimate(
            flops=4 * rows * tokens * width,
            bytes_accessed=4 * width * (tokens + rows) + 6 * rows * tokens,
            transcendentals=0,
        ),
        compiler_params=pltpu.CompilerParams(vmem_limit_bytes=32 * 1024 * 1024),
    )(told, *blocks)


def pick(picking, tokens):
    return jnp.dot(picking, tokens, preferred_element_type=jnp.float32).astype(jnp.bfloat16)


def combine_kernel(weighing, rows, *outs):
    total = jnp.dot(
        jnp.transpose(weighing[...]), rows[...], preferred_element_type=jnp.float32
    ).astype(jnp.bfloat16)
    at = 0
    for out in outs:
        out[...] = total[at : at + out.shape[0], :]
        at += out.shape[0]


def combine(weighing, rows, heights):
    whole = pl.BlockSpec(memory_space=pltpu.VMEM)
    return pl.pallas_call(
        combine_kernel,
        in_specs=[whole] * 2,
        out_specs=[whole] * len(heights),
        out_shape=[pltpu.HBM((height, rows.shape[1]), jnp.bfloat16) for height in heights],
        cost_estimate=pl.CostEstimate(
            flops=2 * weighing.size * rows.shape[1],
            bytes_accessed=2 * (weighing.size + rows.size + sum(heights) * rows.shape[1]),
            transcendentals=0,
        ),
        compiler_params=pltpu.CompilerParams(vmem_limit_bytes=24 * 1024 * 1024),
    )(weighing, rows)


def start_kernel(forward, edge, stored, gain, info, out):
    width = edge.shape[1]
    kept = stored[...].astype(jnp.float32)
    kept_scale = lax.rsqrt(jnp.mean(kept * kept, axis=-1, keepdims=True) + epsilon)
    kept = (kept * kept_scale * gain[...]).astype(jnp.bfloat16)
    out[:, 2 * width :] = info[...]

    @pl.when(forward[0] == 1)
    def _():
        fresh = edge[...].astype(jnp.float32)
        scale = lax.rsqrt(jnp.mean(fresh * fresh, axis=-1, keepdims=True) + epsilon)
        out[:, :width] = (fresh * scale * gain[...]).astype(jnp.bfloat16)
        out[:, width : 2 * width] = kept

    @pl.when(forward[0] != 1)
    def _():
        out[:, :width] = kept
        out[:, width : 2 * width] = edge[...]


def starting_block(forward, edge, stored, gain, info):
    whole = pl.BlockSpec(memory_space=pltpu.VMEM)
    tokens, width = edge.shape
    return pl.pallas_call(
        start_kernel,
        in_specs=[pl.BlockSpec(memory_space=pltpu.SMEM)] + [whole] * 4,
        out_specs=whole,
        out_shape=pltpu.HBM((tokens, 2 * width + info.shape[1]), jnp.bfloat16),
        compiler_params=pltpu.CompilerParams(vmem_limit_bytes=16 * 1024 * 1024),
    )(forward, edge, stored, gain.reshape(1, -1), info)


def normalize(inputs, gain_row):
    widened = inputs.astype(jnp.float32)
    scaling = lax.rsqrt(jnp.mean(widened * widened, axis=-1, keepdims=True) + epsilon)
    return (widened, scaling, (widened * scaling * gain_row).astype(jnp.bfloat16))


def transposed(left, right):
    return lax.dot_general(
        left, right, (((1,), (1,)), ((), ())), preferred_element_type=jnp.float32
    )


def expert_kernel(
    first_at, second_at, forward_from, flag, first, second, w_gate, w_up, w_down, out, *scratch
):
    first_rows, second_rows, gate, up, down, made, done = scratch
    rows, width = first_rows.shape
    into = (
        (first.at[:, pl.ds(first_at * width, width)], first_rows),
        (second.at[:, pl.ds(second_at * width, width)], second_rows),
        (w_gate, gate),
        (w_up, up),
        (w_down, down),
    )
    copies = [
        pltpu.make_async_copy(source, target, done.at[i]) for i, (source, target) in enumerate(into)
    ]
    for copy in copies[:3]:
        copy.start()
    for copy in copies[:3]:
        copy.wait()
    for copy in copies[3:]:
        copy.start()
    forward = flag[0] == 1
    piece = width // 4
    given = [
        pltpu.make_async_copy(made.at[:, part], out.at[:, part], done.at[5 + i])
        for i, part in enumerate(pl.ds(i * piece, piece) for i in range(4))
    ]

    @pl.when(forward)
    def _():
        taken = (first_rows, second_rows)[forward_from][...]
        gate_part = jnp.dot(taken, gate[...], preferred_element_type=jnp.float32)
        copies[3].wait()
        up_part = jnp.dot(taken, up[...], preferred_element_type=jnp.float32)
        hidden = (gate_part * jax.nn.sigmoid(gate_part) * up_part).astype(jnp.bfloat16)
        copies[4].wait()
        for i, copy in enumerate(given):
            part = slice(i * piece, (i + 1) * piece)
            total = jnp.dot(hidden, down[:, part], preferred_element_type=jnp.float32)
            made[:, part] = total.astype(jnp.bfloat16)
            copy.start()

    @pl.when(jnp.logical_not(forward))
    def _():
        taken = first_rows[...]
        gate_part = jnp.dot(taken, gate[...], preferred_element_type=jnp.float32)
        copies[3].wait()
        up_part = jnp.dot(taken, up[...], preferred_element_type=jnp.float32)
        copies[4].wait()
        hidden_grad = transposed(second_rows[...], down[...])
        sigmoid_part = jax.nn.sigmoid(gate_part)
        activated = gate_part * sigmoid_part
        slope = sigmoid_part * (1.0 + gate_part * (1.0 - sigmoid_part))
        gate_grad = (hidden_grad * up_part * slope).astype(jnp.bfloat16)
        up_grad = (hidden_grad * activated).astype(jnp.bfloat16)
        for i, copy in enumerate(given):
            part = slice(i * piece, (i + 1) * piece)
            total = transposed(gate_grad, gate[part, :]) + transposed(up_grad, up[part, :])
            made[:, part] = total.astype(jnp.bfloat16)
            copy.start()

    for copy in given:
        copy.wait()


def apply_expert(flag, first, first_at, second, second_at, forward_from, weights):
    rows, (width, inner) = first.shape[0], weights[0].shape
    weights = [pltpu.with_memory_space_constraint(w, pltpu.HBM) for w in weights]
    return pl.pallas_call(
        functools.partial(expert_kernel, first_at, second_at, forward_from),
        in_specs=[pl.BlockSpec(memory_space=pltpu.SMEM)] + [pl.BlockSpec(memory_space=pl.ANY)] * 5,
        out_specs=pl.BlockSpec(memory_space=pl.ANY),
        out_shape=pltpu.HBM((rows, width), jnp.bfloat16),
        scratch_shapes=[pltpu.VMEM((rows, width), jnp.bfloat16)] * 2
        + [pltpu.VMEM(w.shape, w.dtype) for w in weights]
        + [pltpu.VMEM((rows, width), jnp.bfloat16), pltpu.SemaphoreType.DMA((9,))],
        cost_estimate=pl.CostEstimate(
            flops=10 * rows * width * inner,
            bytes_accessed=6 * width * (rows + inner),
            transcendentals=rows * inner,
        ),
        compiler_params=pltpu.CompilerParams(vmem_limit_bytes=56 * 1024 * 1024),
    )(flag, first, second, *weights)


def finish(widened, scaling, gain_row, upstream, summed, forward_flag):
    forward_out = widened + summed
    scaled = summed * gain_row
    inner_mean = jnp.mean(scaled * widened, axis=-1, keepdims=True)
    cubed = scaling * scaling * scaling
    backward_out = upstream.astype(jnp.float32) + scaling * scaled - widened * cubed * inner_mean
    return jnp.where(forward_flag, forward_out, backward_out).astype(jnp.bfloat16)


def stack(blocks, chunk):
    return jnp.concatenate([blocks[k] for k in chunk], axis=0)


def after(first, then):
    return lax.optimization_barrier((first, then))


def returned(outcomes, weighings, code_sum):
    near, far = outcomes
    far_back = exchange(far)
    far_back, near = after(far_back, near)
    near_back = exchange(near)
    parts = dict(zip(CHUNKS[0], combine(weighings[0], near_back, [TOKENS] * len(CHUNKS[0]))))
    *rest, first, last = combine(
        weighings[1], far_back, [TOKENS] * (len(CHUNKS[1]) - 1) + [TOKENS // 2] * 2
    )
    parts.update(zip(CHUNKS[1], (*rest, (first, last))))
    return sum_ring(parts) / code_sum


def body(boundary, saved, norm_gain, gate_weight, up_weight, down_weight, routes, gate_codes):
    first_segment = lax.axis_index("segment") == 0
    later_forward = jnp.logical_not(first_segment)
    width = boundary.shape[2]
    weights = (gate_weight[0, 0], up_weight[0, 0], down_weight[0, 0])
    gain_row = norm_gain[0]
    edge_rows = boundary[0]
    stored = saved[0]
    route_now = jnp.where(first_segment, routes[0, 0], routes[0, 1])
    codes_now = jnp.where(first_segment, gate_codes[0, 0], gate_codes[0, 1])
    route_next = jnp.where(first_segment, routes[0, 1], routes[0, 0])
    codes_next = jnp.where(first_segment, gate_codes[0, 1], gate_codes[0, 0])
    sum_now = jnp.sum(codes_now.astype(jnp.float32), axis=-1, keepdims=True)
    sum_next = jnp.sum(codes_next.astype(jnp.float32), axis=-1, keepdims=True)
    top = route_now.shape[1]
    info = jnp.concatenate((route_now, codes_now, route_next, codes_next), axis=1)
    info = jnp.pad(info.astype(jnp.bfloat16), ((0, 0), (0, 128 - 4 * top)))

    inputs_now = jnp.where(first_segment, edge_rows, stored)
    widened, scaling, _ = normalize(inputs_now, gain_row)

    forward_first = first_segment.astype(jnp.int32).reshape(1)
    told = jnp.stack((lax.axis_index(RING), first_segment.astype(jnp.int32)))

    blocks = gather_near(starting_block(forward_first, edge_rows, stored, gain_row, info))
    pairs, place_next, weigh_now, weigh_next = [], [], [], []
    for chunk in CHUNKS:
        if pairs:
            blocks = gather_far(blocks)
        picked, pick_next, by_now, by_next = pick_both(
            told, [blocks[k] for k in chunk], top, width
        )
        if pairs:
            pairs[-1], picked = after(pairs[-1], picked)
        else:
            picked, blocks = after(picked, blocks)
        pairs.append(exchange(picked))
        place_next.append(pick_next)
        weigh_now.append(by_now)
        weigh_next.append(by_next)
    outcomes = [apply_expert(forward_first, pair, 0, pair, 1, 0, weights) for pair in pairs]
    summed = returned(outcomes, weigh_now, sum_now)
    produced = finish(widened, scaling, gain_row, edge_rows, summed, first_segment)

    arrived = lax.ppermute(produced, "segment", [(0, 1), (1, 0)])
    inputs_next = jnp.where(first_segment, stored, arrived)
    widened_next, scaling_next, normed_next = normalize(inputs_next, gain_row)
    member_blocks = gather_far(gather_near(jnp.where(first_segment, arrived, normed_next)))
    landed = []
    for i, chunk in enumerate(CHUNKS):
        picked = pick(place_next[i], stack(member_blocks, chunk))
        if landed:
            landed[-1], picked = after(landed[-1], picked)
        landed.append(exchange(picked))
    outcomes = [
        apply_expert(1 - forward_first, pair, 1, rows, 0, 1, weights)
        for pair, rows in zip(pairs, landed)
    ]
    summed = returned(outcomes, weigh_next, sum_next)
    result = finish(widened_next, scaling_next, gain_row, arrived, summed, later_forward)
    return result[None]


def solution(mesh):
    finer = Mesh(
        mesh.devices.reshape(mesh.shape["segment"], 4, 2, 8, 2),
        ("segment", "expert_0", "expert_1", "expert_2", "expert_3"),
    )
    placed = (
        P("segment", EXPERT, None),
        P("segment", EXPERT, None),
        P("segment", None),
        P("segment", EXPERT, None, None),
        P("segment", EXPERT, None, None),
        P("segment", EXPERT, None, None),
        P("segment", None, EXPERT, None),
        P("segment", None, EXPERT, None),
    )
    return jax.shard_map(
        body, mesh=finer, in_specs=placed, out_specs=P("segment", EXPERT, None), check_vma=False
    )
```

```python
import functools

import jax
import jax.numpy as jnp
from jax import lax
from jax.experimental import pallas as pl
from jax.experimental.pallas import tpu as pltpu
from jax.sharding import Mesh
from jax.sharding import PartitionSpec as P

EXPERT = ("expert_0", "expert_1", "expert_2", "expert_3")
PLANE = ("expert_0", "expert_1", "expert_3")
RING = "expert_2"

CHUNKS = ((0, -1, 1, -2), (2, -3, 3, 4))
CAPACITY = 6
TOKENS = 64

epsilon = 1e-06


def step_ring(block, step):
    count = lax.axis_size(RING)
    return lax.ppermute(block, RING, [(i, (i + step) % count) for i in range(count)])


def gather_near(own):
    blocks = {0: own}
    for distance in (1, 2):
        blocks[-distance] = step_ring(blocks[1 - distance], 1)
        blocks[distance] = step_ring(blocks[distance - 1], -1)
    return blocks


def gather_far(blocks):
    half = blocks[0].shape[0] // 2
    up, down = step_ring(blocks[-2], 1), step_ring(blocks[2], -1)
    last = jnp.concatenate((step_ring(up[:half], 1), step_ring(down[half:], -1)), axis=0)
    return {**blocks, -3: up, 3: down, 4: last}


def add(part, arrived):
    return (part.astype(jnp.float32) + arrived.astype(jnp.float32)).astype(jnp.bfloat16)


def exchange(rows):
    count = lax.axis_size(PLANE)
    parts = rows.reshape(count, -1, rows.shape[-1])
    moved = lax.all_to_all(parts, PLANE, split_axis=0, concat_axis=0, tiled=True)
    return moved.reshape(rows.shape)


def one_hots(ids, codes, first_chip, ring, peers):
    width = ids.shape[1]
    blocks = width // TOKENS
    plane = lax.broadcasted_iota(jnp.int32, (peers, 1), 0)
    named = ((((plane >> 1) * ring + first_chip) << 1) + (plane & 1)).astype(jnp.float32)
    member = jnp.zeros((peers, width), jnp.float32)
    code = jnp.zeros((peers, width), jnp.float32)
    for k in range(ids.shape[0]):
        hit = ids[k : k + 1, :] == named
        member = jnp.where(hit, 1.0, member)
        code = jnp.where(hit, codes[k : k + 1, :], code)
    row = lax.broadcasted_iota(jnp.int32, (width, width), 0)
    column = lax.broadcasted_iota(jnp.int32, (width, width), 1)
    earlier = jnp.where((row // TOKENS == column // TOKENS) & (row < column), 1.0, 0.0)
    rank = jnp.dot(
        member.astype(jnp.bfloat16),
        earlier.astype(jnp.bfloat16),
        preferred_element_type=jnp.float32,
    )
    block = lax.broadcasted_iota(jnp.int32, (1, width), 1) // TOKENS
    key = jnp.where(member > 0.0, (block * CAPACITY).astype(jnp.float32) + rank, -1.0)
    rows = blocks * CAPACITY
    place = lax.broadcasted_iota(jnp.int32, (peers, rows, width), 1).astype(jnp.float32)
    found = jnp.broadcast_to(key[:, None, :], (peers, rows, width)) == place
    picking = jnp.where(found, 1.0, 0.0)
    weighing = jnp.where(found, jnp.broadcast_to(code[:, None, :], (peers, rows, width)), 0.0)
    return (picking.reshape(-1, width), weighing.reshape(-1, width))


def pick_kernel(top, ring, peers, told, *refs):
    count = len(refs) - 5
    blocks, (picked, next_out, by_now_out, by_next_out, held) = refs[:count], refs[count:]
    width = picked.shape[1] // 2
    for i, block in enumerate(blocks):
        held[i * TOKENS : (i + 1) * TOKENS, :] = block[...]
    info = jnp.transpose(held[:, 2 * width :].astype(jnp.float32))
    ids_now, codes_now, ids_next, codes_next = (info[i * top : (i + 1) * top, :] for i in range(4))
    pick_now, by_now = one_hots(ids_now, codes_now, told[0], ring, peers)
    pick_next, by_next = one_hots(ids_next, codes_next, told[0], ring, peers)
    early = jnp.where(told[1] == 1, pick_next, pick_now).astype(jnp.bfloat16)
    pick_now = pick_now.astype(jnp.bfloat16)
    picked[:, :width] = jnp.dot(
        pick_now, held[:, :width], preferred_element_type=jnp.float32
    ).astype(jnp.bfloat16)
    picked[:, width:] = jnp.dot(
        early, held[:, width : 2 * width], preferred_element_type=jnp.float32
    ).astype(jnp.bfloat16)
    next_out[...] = pick_next.astype(jnp.bfloat16)
    by_now_out[...] = by_now.astype(jnp.bfloat16)
    by_next_out[...] = by_next.astype(jnp.bfloat16)


def pick_both(told, blocks, top, width):
    ring, peers = lax.axis_size(RING), lax.axis_size(PLANE)
    tokens = len(blocks) * TOKENS
    rows = peers * len(blocks) * CAPACITY
    whole = pl.BlockSpec(memory_space=pltpu.VMEM)
    kept = pltpu.HBM((rows, tokens), jnp.bfloat16)
    blocks = [pltpu.with_memory_space_constraint(block, pltpu.HBM) for block in blocks]
    return pl.pallas_call(
        functools.partial(pick_kernel, top, ring, peers),
        in_specs=[pl.BlockSpec(memory_space=pltpu.SMEM)] + [whole] * len(blocks),
        out_specs=[whole] * 4,
        out_shape=[pltpu.HBM((rows, 2 * width), jnp.bfloat16), kept, kept, kept],
        scratch_shapes=[pltpu.VMEM((tokens, blocks[0].shape[1]), jnp.bfloat16)],
        cost_estimate=pl.CostEstimate(
            flops=4 * rows * tokens * width,
            bytes_accessed=4 * width * (tokens + rows) + 6 * rows * tokens,
            transcendentals=0,
        ),
        compiler_params=pltpu.CompilerParams(vmem_limit_bytes=32 * 1024 * 1024),
    )(told, *blocks)


def pick(picking, tokens):
    return jnp.dot(picking, tokens, preferred_element_type=jnp.float32).astype(jnp.bfloat16)


def combine_kernel(added, weighing, rows, *refs):
    arrived, outs = refs[: len(added)], refs[len(added) :]
    total = jnp.dot(jnp.transpose(weighing[...]), rows[...], preferred_element_type=jnp.float32)
    at = 0
    for i, out in enumerate(outs):
        piece = total[at : at + out.shape[0], :]
        if i in added:
            piece = piece + arrived[added.index(i)][...].astype(jnp.float32)
        out[...] = piece.astype(jnp.bfloat16)
        at += out.shape[0]


def combine(weighing, rows, heights, arrived=None):
    arrived = arrived or {}
    whole = pl.BlockSpec(memory_space=pltpu.VMEM)
    return pl.pallas_call(
        functools.partial(combine_kernel, tuple(arrived)),
        in_specs=[whole] * (2 + len(arrived)),
        out_specs=[whole] * len(heights),
        out_shape=[pltpu.HBM((height, rows.shape[1]), jnp.bfloat16) for height in heights],
        cost_estimate=pl.CostEstimate(
            flops=2 * weighing.size * rows.shape[1],
            bytes_accessed=2 * (weighing.size + rows.size + sum(heights) * rows.shape[1]),
            transcendentals=0,
        ),
        compiler_params=pltpu.CompilerParams(vmem_limit_bytes=24 * 1024 * 1024),
    )(weighing, rows, *arrived.values())


def start_kernel(forward, edge, stored, gain, info, out):
    width = edge.shape[1]
    kept = stored[...].astype(jnp.float32)
    kept_scale = lax.rsqrt(jnp.mean(kept * kept, axis=-1, keepdims=True) + epsilon)
    kept = (kept * kept_scale * gain[...]).astype(jnp.bfloat16)
    out[:, 2 * width :] = info[...]

    @pl.when(forward[0] == 1)
    def _():
        fresh = edge[...].astype(jnp.float32)
        scale = lax.rsqrt(jnp.mean(fresh * fresh, axis=-1, keepdims=True) + epsilon)
        out[:, :width] = (fresh * scale * gain[...]).astype(jnp.bfloat16)
        out[:, width : 2 * width] = kept

    @pl.when(forward[0] != 1)
    def _():
        out[:, :width] = kept
        out[:, width : 2 * width] = edge[...]


def starting_block(forward, edge, stored, gain, info):
    whole = pl.BlockSpec(memory_space=pltpu.VMEM)
    tokens, width = edge.shape
    return pl.pallas_call(
        start_kernel,
        in_specs=[pl.BlockSpec(memory_space=pltpu.SMEM)] + [whole] * 4,
        out_specs=whole,
        out_shape=pltpu.HBM((tokens, 2 * width + info.shape[1]), jnp.bfloat16),
        compiler_params=pltpu.CompilerParams(vmem_limit_bytes=16 * 1024 * 1024),
    )(forward, edge, stored, gain.reshape(1, -1), info)


def normalize(inputs, gain_row):
    widened = inputs.astype(jnp.float32)
    scaling = lax.rsqrt(jnp.mean(widened * widened, axis=-1, keepdims=True) + epsilon)
    return (widened, scaling, (widened * scaling * gain_row).astype(jnp.bfloat16))


def transposed(left, right):
    return lax.dot_general(
        left, right, (((1,), (1,)), ((), ())), preferred_element_type=jnp.float32
    )


def expert_kernel(
    first_at, second_at, forward_from, flag, first, second, w_gate, w_up, w_down, out, *scratch
):
    first_rows, second_rows, gate, up, down, made, done = scratch
    rows, width = first_rows.shape
    into = (
        (first.at[:, pl.ds(first_at * width, width)], first_rows),
        (second.at[:, pl.ds(second_at * width, width)], second_rows),
        (w_gate, gate),
        (w_up, up),
        (w_down, down),
    )
    copies = [
        pltpu.make_async_copy(source, target, done.at[i]) for i, (source, target) in enumerate(into)
    ]
    for copy in copies[:3]:
        copy.start()
    for copy in copies[:3]:
        copy.wait()
    for copy in copies[3:]:
        copy.start()
    forward = flag[0] == 1
    piece = width // 4
    given = [
        pltpu.make_async_copy(made.at[:, part], out.at[:, part], done.at[5 + i])
        for i, part in enumerate(pl.ds(i * piece, piece) for i in range(4))
    ]

    @pl.when(forward)
    def _():
        taken = (first_rows, second_rows)[forward_from][...]
        gate_part = jnp.dot(taken, gate[...], preferred_element_type=jnp.float32)
        copies[3].wait()
        up_part = jnp.dot(taken, up[...], preferred_element_type=jnp.float32)
        hidden = (gate_part * jax.nn.sigmoid(gate_part) * up_part).astype(jnp.bfloat16)
        copies[4].wait()
        for i, copy in enumerate(given):
            part = slice(i * piece, (i + 1) * piece)
            total = jnp.dot(hidden, down[:, part], preferred_element_type=jnp.float32)
            made[:, part] = total.astype(jnp.bfloat16)
            copy.start()

    @pl.when(jnp.logical_not(forward))
    def _():
        taken = first_rows[...]
        gate_part = jnp.dot(taken, gate[...], preferred_element_type=jnp.float32)
        copies[3].wait()
        up_part = jnp.dot(taken, up[...], preferred_element_type=jnp.float32)
        copies[4].wait()
        hidden_grad = transposed(second_rows[...], down[...])
        sigmoid_part = jax.nn.sigmoid(gate_part)
        activated = gate_part * sigmoid_part
        slope = sigmoid_part * (1.0 + gate_part * (1.0 - sigmoid_part))
        gate_grad = (hidden_grad * up_part * slope).astype(jnp.bfloat16)
        up_grad = (hidden_grad * activated).astype(jnp.bfloat16)
        for i, copy in enumerate(given):
            part = slice(i * piece, (i + 1) * piece)
            total = transposed(gate_grad, gate[part, :]) + transposed(up_grad, up[part, :])
            made[:, part] = total.astype(jnp.bfloat16)
            copy.start()

    for copy in given:
        copy.wait()


def apply_expert(flag, first, first_at, second, second_at, forward_from, weights):
    rows, (width, inner) = first.shape[0], weights[0].shape
    weights = [pltpu.with_memory_space_constraint(w, pltpu.HBM) for w in weights]
    return pl.pallas_call(
        functools.partial(expert_kernel, first_at, second_at, forward_from),
        in_specs=[pl.BlockSpec(memory_space=pltpu.SMEM)] + [pl.BlockSpec(memory_space=pl.ANY)] * 5,
        out_specs=pl.BlockSpec(memory_space=pl.ANY),
        out_shape=pltpu.HBM((rows, width), jnp.bfloat16),
        scratch_shapes=[pltpu.VMEM((rows, width), jnp.bfloat16)] * 2
        + [pltpu.VMEM(w.shape, w.dtype) for w in weights]
        + [pltpu.VMEM((rows, width), jnp.bfloat16), pltpu.SemaphoreType.DMA((9,))],
        cost_estimate=pl.CostEstimate(
            flops=10 * rows * width * inner,
            bytes_accessed=6 * width * (rows + inner),
            transcendentals=rows * inner,
        ),
        compiler_params=pltpu.CompilerParams(vmem_limit_bytes=56 * 1024 * 1024),
    )(flag, first, second, *weights)


def finish(widened, scaling, gain_row, upstream, summed, forward_flag):
    forward_out = widened + summed
    scaled = summed * gain_row
    inner_mean = jnp.mean(scaled * widened, axis=-1, keepdims=True)
    cubed = scaling * scaling * scaling
    backward_out = upstream.astype(jnp.float32) + scaling * scaled - widened * cubed * inner_mean
    return jnp.where(forward_flag, forward_out, backward_out).astype(jnp.bfloat16)


def stack(blocks, chunk):
    return jnp.concatenate([blocks[k] for k in chunk], axis=0)


def after(first, then):
    return lax.optimization_barrier((first, then))


def returned(outcomes, weighings, code_sum):
    near, far = outcomes
    far_back = exchange(far)
    far_back, near = after(far_back, near)
    near_back = exchange(near)
    half = TOKENS // 2
    up_2, down_3, up_3, first, last = combine(weighings[1], far_back, [TOKENS] * 3 + [half] * 2)
    up, down = step_ring(first, 1), step_ring(last, -1)
    up = jnp.concatenate((add(up_3[:half], up), up_3[half:]), axis=0)
    down = jnp.concatenate((down_3[:half], add(down_3[half:], down)), axis=0)
    up = step_ring(add(up_2, step_ring(up, 1)), 1)
    down = step_ring(down, -1)
    own, down_1, up, down = combine(weighings[0], near_back, [TOKENS] * 4, {2: up, 3: down})
    up = step_ring(up, 1)
    down = step_ring(add(down_1, step_ring(down, -1)), -1)
    return sum(part.astype(jnp.float32) for part in (own, up, down)) / code_sum


def body(boundary, saved, norm_gain, gate_weight, up_weight, down_weight, routes, gate_codes):
    first_segment = lax.axis_index("segment") == 0
    later_forward = jnp.logical_not(first_segment)
    width = boundary.shape[2]
    weights = (gate_weight[0, 0], up_weight[0, 0], down_weight[0, 0])
    gain_row = norm_gain[0]
    edge_rows = boundary[0]
    stored = saved[0]
    route_now = jnp.where(first_segment, routes[0, 0], routes[0, 1])
    codes_now = jnp.where(first_segment, gate_codes[0, 0], gate_codes[0, 1])
    route_next = jnp.where(first_segment, routes[0, 1], routes[0, 0])
    codes_next = jnp.where(first_segment, gate_codes[0, 1], gate_codes[0, 0])
    sum_now = jnp.sum(codes_now.astype(jnp.float32), axis=-1, keepdims=True)
    sum_next = jnp.sum(codes_next.astype(jnp.float32), axis=-1, keepdims=True)
    top = route_now.shape[1]
    info = jnp.concatenate((route_now, codes_now, route_next, codes_next), axis=1)
    info = jnp.pad(info.astype(jnp.bfloat16), ((0, 0), (0, 128 - 4 * top)))

    inputs_now = jnp.where(first_segment, edge_rows, stored)
    widened, scaling, _ = normalize(inputs_now, gain_row)

    forward_first = first_segment.astype(jnp.int32).reshape(1)
    told = jnp.stack((lax.axis_index(RING), first_segment.astype(jnp.int32)))

    blocks = gather_near(starting_block(forward_first, edge_rows, stored, gain_row, info))
    pairs, place_next, weigh_now, weigh_next = [], [], [], []
    for chunk in CHUNKS:
        if pairs:
            blocks = gather_far(blocks)
        picked, pick_next, by_now, by_next = pick_both(
            told, [blocks[k] for k in chunk], top, width
        )
        if pairs:
            pairs[-1], picked = after(pairs[-1], picked)
        else:
            picked, blocks = after(picked, blocks)
        pairs.append(exchange(picked))
        place_next.append(pick_next)
        weigh_now.append(by_now)
        weigh_next.append(by_next)
    outcomes = [apply_expert(forward_first, pair, 0, pair, 1, 0, weights) for pair in pairs]
    summed = returned(outcomes, weigh_now, sum_now)
    produced = finish(widened, scaling, gain_row, edge_rows, summed, first_segment)

    arrived = lax.ppermute(produced, "segment", [(0, 1), (1, 0)])
    inputs_next = jnp.where(first_segment, stored, arrived)
    widened_next, scaling_next, normed_next = normalize(inputs_next, gain_row)
    member_blocks = gather_far(gather_near(jnp.where(first_segment, arrived, normed_next)))
    landed = []
    for i, chunk in enumerate(CHUNKS):
        picked = pick(place_next[i], stack(member_blocks, chunk))
        if landed:
            landed[-1], picked = after(landed[-1], picked)
        landed.append(exchange(picked))
    outcomes = [
        apply_expert(1 - forward_first, pair, 1, rows, 0, 1, weights)
        for pair, rows in zip(pairs, landed)
    ]
    summed = returned(outcomes, weigh_next, sum_next)
    result = finish(widened_next, scaling_next, gain_row, arrived, summed, later_forward)
    return result[None]


def solution(mesh):
    finer = Mesh(
        mesh.devices.reshape(mesh.shape["segment"], 4, 2, 8, 2),
        ("segment", "expert_0", "expert_1", "expert_2", "expert_3"),
    )
    placed = (
        P("segment", EXPERT, None),
        P("segment", EXPERT, None),
        P("segment", None),
        P("segment", EXPERT, None, None),
        P("segment", EXPERT, None, None),
        P("segment", EXPERT, None, None),
        P("segment", None, EXPERT, None),
        P("segment", None, EXPERT, None),
    )
    return jax.shard_map(
        body, mesh=finer, in_specs=placed, out_specs=P("segment", EXPERT, None), check_vma=False
    )
```

```python
import functools

import jax
import jax.numpy as jnp
from jax import lax
from jax.experimental import pallas as pl
from jax.experimental.pallas import tpu as pltpu
from jax.sharding import Mesh
from jax.sharding import PartitionSpec as P

EXPERT = ("expert_0", "expert_1", "expert_2", "expert_3")
PLANE = ("expert_0", "expert_1", "expert_3")
RING = "expert_2"

CHUNKS = ((0, -1, 1, -2), (2, -3, 3, 4))
CAPACITY = 6
TOKENS = 64

epsilon = 1e-06


def step_ring(block, step):
    count = lax.axis_size(RING)
    return lax.ppermute(block, RING, [(i, (i + step) % count) for i in range(count)])


def gather_near(own):
    blocks = {0: own}
    for distance in (1, 2):
        blocks[-distance] = step_ring(blocks[1 - distance], 1)
        blocks[distance] = step_ring(blocks[distance - 1], -1)
    return blocks


def gather_far(blocks):
    half = blocks[0].shape[0] // 2
    up, down = step_ring(blocks[-2], 1), step_ring(blocks[2], -1)
    last = jnp.concatenate((step_ring(up[:half], 1), step_ring(down[half:], -1)), axis=0)
    return {**blocks, -3: up, 3: down, 4: last}


def add(part, arrived):
    return (part.astype(jnp.float32) + arrived.astype(jnp.float32)).astype(jnp.bfloat16)


def sum_ring(parts):
    first, last = parts[4]
    half = first.shape[0]
    up, down = step_ring(first, 1), step_ring(last, -1)
    up = jnp.concatenate((add(parts[3][:half], up), parts[3][half:]), axis=0)
    down = jnp.concatenate((parts[-3][:half], add(parts[-3][half:], down)), axis=0)
    for distance in (2, 1):
        up = add(parts[distance], step_ring(up, 1))
        down = add(parts[-distance], step_ring(down, -1))
    up, down = step_ring(up, 1), step_ring(down, -1)
    return sum(part.astype(jnp.float32) for part in (parts[0], up, down))


def exchange(rows):
    count = lax.axis_size(PLANE)
    parts = rows.reshape(count, -1, rows.shape[-1])
    moved = lax.all_to_all(parts, PLANE, split_axis=0, concat_axis=0, tiled=True)
    return moved.reshape(rows.shape)


def one_hots(ids, codes, first_chip, ring, peers):
    width = ids.shape[1]
    blocks = width // TOKENS
    plane = lax.broadcasted_iota(jnp.int32, (peers, 1), 0)
    named = ((((plane >> 1) * ring + first_chip) << 1) + (plane & 1)).astype(jnp.float32)
    member = jnp.zeros((peers, width), jnp.float32)
    code = jnp.zeros((peers, width), jnp.float32)
    for k in range(ids.shape[0]):
        hit = ids[k : k + 1, :] == named
        member = jnp.where(hit, 1.0, member)
        code = jnp.where(hit, codes[k : k + 1, :], code)
    row = lax.broadcasted_iota(jnp.int32, (width, width), 0)
    column = lax.broadcasted_iota(jnp.int32, (width, width), 1)
    earlier = jnp.where((row // TOKENS == column // TOKENS) & (row < column), 1.0, 0.0)
    rank = jnp.dot(
        member.astype(jnp.bfloat16),
        earlier.astype(jnp.bfloat16),
        preferred_element_type=jnp.float32,
    )
    block = lax.broadcasted_iota(jnp.int32, (1, width), 1) // TOKENS
    key = jnp.where(member > 0.0, (block * CAPACITY).astype(jnp.float32) + rank, -1.0)
    rows = blocks * CAPACITY
    place = lax.broadcasted_iota(jnp.int32, (peers, rows, width), 1).astype(jnp.float32)
    found = jnp.broadcast_to(key[:, None, :], (peers, rows, width)) == place
    picking = jnp.where(found, 1.0, 0.0)
    weighing = jnp.where(found, jnp.broadcast_to(code[:, None, :], (peers, rows, width)), 0.0)
    return (picking.reshape(-1, width), weighing.reshape(-1, width))


def pick_kernel(top, ring, peers, told, *refs):
    count = len(refs) - 5
    blocks, (picked, next_out, by_now_out, by_next_out, held) = refs[:count], refs[count:]
    width = picked.shape[1] // 2
    for i, block in enumerate(blocks):
        held[i * TOKENS : (i + 1) * TOKENS, :] = block[...]
    info = jnp.transpose(held[:, 2 * width :].astype(jnp.float32))
    ids_now, codes_now, ids_next, codes_next = (info[i * top : (i + 1) * top, :] for i in range(4))
    pick_now, by_now = one_hots(ids_now, codes_now, told[0], ring, peers)
    pick_next, by_next = one_hots(ids_next, codes_next, told[0], ring, peers)
    early = jnp.where(told[1] == 1, pick_next, pick_now).astype(jnp.bfloat16)
    pick_now = pick_now.astype(jnp.bfloat16)
    picked[:, :width] = jnp.dot(
        pick_now, held[:, :width], preferred_element_type=jnp.float32
    ).astype(jnp.bfloat16)
    picked[:, width:] = jnp.dot(
        early, held[:, width : 2 * width], preferred_element_type=jnp.float32
    ).astype(jnp.bfloat16)
    next_out[...] = pick_next.astype(jnp.bfloat16)
    by_now_out[...] = by_now.astype(jnp.bfloat16)
    by_next_out[...] = by_next.astype(jnp.bfloat16)


def pick_both(told, blocks, top, width):
    ring, peers = lax.axis_size(RING), lax.axis_size(PLANE)
    tokens = len(blocks) * TOKENS
    rows = peers * len(blocks) * CAPACITY
    whole = pl.BlockSpec(memory_space=pltpu.VMEM)
    kept = pltpu.HBM((rows, tokens), jnp.bfloat16)
    blocks = [pltpu.with_memory_space_constraint(block, pltpu.HBM) for block in blocks]
    return pl.pallas_call(
        functools.partial(pick_kernel, top, ring, peers),
        in_specs=[pl.BlockSpec(memory_space=pltpu.SMEM)] + [whole] * len(blocks),
        out_specs=[whole] * 4,
        out_shape=[pltpu.HBM((rows, 2 * width), jnp.bfloat16), kept, kept, kept],
        scratch_shapes=[pltpu.VMEM((tokens, blocks[0].shape[1]), jnp.bfloat16)],
        cost_estimate=pl.CostEstimate(
            flops=4 * rows * tokens * width,
            bytes_accessed=4 * width * (tokens + rows) + 6 * rows * tokens,
            transcendentals=0,
        ),
        compiler_params=pltpu.CompilerParams(vmem_limit_bytes=32 * 1024 * 1024),
    )(told, *blocks)


def pick(picking, tokens):
    return jnp.dot(picking, tokens, preferred_element_type=jnp.float32).astype(jnp.bfloat16)


def combine_kernel(weighing, rows, *outs):
    total = jnp.dot(
        jnp.transpose(weighing[...]), rows[...], preferred_element_type=jnp.float32
    ).astype(jnp.bfloat16)
    at = 0
    for out in outs:
        out[...] = total[at : at + out.shape[0], :]
        at += out.shape[0]


def combine(weighing, rows, heights):
    whole = pl.BlockSpec(memory_space=pltpu.VMEM)
    return pl.pallas_call(
        combine_kernel,
        in_specs=[whole] * 2,
        out_specs=[whole] * len(heights),
        out_shape=[pltpu.HBM((height, rows.shape[1]), jnp.bfloat16) for height in heights],
        cost_estimate=pl.CostEstimate(
            flops=2 * weighing.size * rows.shape[1],
            bytes_accessed=2 * (weighing.size + rows.size + sum(heights) * rows.shape[1]),
            transcendentals=0,
        ),
        compiler_params=pltpu.CompilerParams(vmem_limit_bytes=24 * 1024 * 1024),
    )(weighing, rows)


def start_kernel(forward, edge, stored, gain, info, out):
    width = edge.shape[1]
    kept = stored[...].astype(jnp.float32)
    kept_scale = lax.rsqrt(jnp.mean(kept * kept, axis=-1, keepdims=True) + epsilon)
    kept = (kept * kept_scale * gain[...]).astype(jnp.bfloat16)
    out[:, 2 * width :] = info[...]

    @pl.when(forward[0] == 1)
    def _():
        fresh = edge[...].astype(jnp.float32)
        scale = lax.rsqrt(jnp.mean(fresh * fresh, axis=-1, keepdims=True) + epsilon)
        out[:, :width] = (fresh * scale * gain[...]).astype(jnp.bfloat16)
        out[:, width : 2 * width] = kept

    @pl.when(forward[0] != 1)
    def _():
        out[:, :width] = kept
        out[:, width : 2 * width] = edge[...]


def starting_block(forward, edge, stored, gain, info):
    whole = pl.BlockSpec(memory_space=pltpu.VMEM)
    tokens, width = edge.shape
    edge, stored = (pltpu.with_memory_space_constraint(rows, pltpu.HBM) for rows in (edge, stored))
    return pl.pallas_call(
        start_kernel,
        in_specs=[pl.BlockSpec(memory_space=pltpu.SMEM)] + [whole] * 4,
        out_specs=whole,
        out_shape=pltpu.HBM((tokens, 2 * width + info.shape[1]), jnp.bfloat16),
        compiler_params=pltpu.CompilerParams(vmem_limit_bytes=16 * 1024 * 1024),
    )(forward, edge, stored, gain.reshape(1, -1), info)


def normalize(inputs, gain_row):
    widened = inputs.astype(jnp.float32)
    scaling = lax.rsqrt(jnp.mean(widened * widened, axis=-1, keepdims=True) + epsilon)
    return (widened, scaling, (widened * scaling * gain_row).astype(jnp.bfloat16))


def transposed(left, right):
    return lax.dot_general(
        left, right, (((1,), (1,)), ((), ())), preferred_element_type=jnp.float32
    )


def expert_kernel(
    first_at, second_at, forward_from, flag, first, second, w_gate, w_up, w_down, out, *scratch
):
    first_rows, second_rows, gate, up, down, made, done = scratch
    rows, width = first_rows.shape
    into = (
        (first.at[:, pl.ds(first_at * width, width)], first_rows),
        (second.at[:, pl.ds(second_at * width, width)], second_rows),
        (w_gate, gate),
        (w_up, up),
        (w_down, down),
    )
    copies = [
        pltpu.make_async_copy(source, target, done.at[i]) for i, (source, target) in enumerate(into)
    ]
    for copy in (copies[0], copies[2]):
        copy.start()
    for copy in (copies[0], copies[2]):
        copy.wait()
    for copy in (copies[1], *copies[3:]):
        copy.start()
    forward = flag[0] == 1
    piece = width // 4
    given = [
        pltpu.make_async_copy(made.at[:, part], out.at[:, part], done.at[5 + i])
        for i, part in enumerate(pl.ds(i * piece, piece) for i in range(4))
    ]

    @pl.when(forward)
    def _():
        copies[1].wait()
        taken = (first_rows, second_rows)[forward_from][...]
        gate_part = jnp.dot(taken, gate[...], preferred_element_type=jnp.float32)
        copies[3].wait()
        up_part = jnp.dot(taken, up[...], preferred_element_type=jnp.float32)
        hidden = (gate_part * jax.nn.sigmoid(gate_part) * up_part).astype(jnp.bfloat16)
        copies[4].wait()
        for i, copy in enumerate(given):
            part = slice(i * piece, (i + 1) * piece)
            total = jnp.dot(hidden, down[:, part], preferred_element_type=jnp.float32)
            made[:, part] = total.astype(jnp.bfloat16)
            copy.start()

    @pl.when(jnp.logical_not(forward))
    def _():
        taken = first_rows[...]
        gate_part = jnp.dot(taken, gate[...], preferred_element_type=jnp.float32)
        copies[3].wait()
        up_part = jnp.dot(taken, up[...], preferred_element_type=jnp.float32)
        copies[1].wait()
        copies[4].wait()
        hidden_grad = transposed(second_rows[...], down[...])
        sigmoid_part = jax.nn.sigmoid(gate_part)
        activated = gate_part * sigmoid_part
        slope = sigmoid_part * (1.0 + gate_part * (1.0 - sigmoid_part))
        gate_grad = (hidden_grad * up_part * slope).astype(jnp.bfloat16)
        up_grad = (hidden_grad * activated).astype(jnp.bfloat16)
        for i, copy in enumerate(given):
            part = slice(i * piece, (i + 1) * piece)
            total = transposed(gate_grad, gate[part, :]) + transposed(up_grad, up[part, :])
            made[:, part] = total.astype(jnp.bfloat16)
            copy.start()

    for copy in given:
        copy.wait()


def apply_expert(flag, first, first_at, second, second_at, forward_from, weights):
    rows, (width, inner) = first.shape[0], weights[0].shape
    weights = [pltpu.with_memory_space_constraint(w, pltpu.HBM) for w in weights]
    return pl.pallas_call(
        functools.partial(expert_kernel, first_at, second_at, forward_from),
        in_specs=[pl.BlockSpec(memory_space=pltpu.SMEM)] + [pl.BlockSpec(memory_space=pl.ANY)] * 5,
        out_specs=pl.BlockSpec(memory_space=pl.ANY),
        out_shape=pltpu.HBM((rows, width), jnp.bfloat16),
        scratch_shapes=[pltpu.VMEM((rows, width), jnp.bfloat16)] * 2
        + [pltpu.VMEM(w.shape, w.dtype) for w in weights]
        + [pltpu.VMEM((rows, width), jnp.bfloat16), pltpu.SemaphoreType.DMA((9,))],
        cost_estimate=pl.CostEstimate(
            flops=10 * rows * width * inner,
            bytes_accessed=6 * width * (rows + inner),
            transcendentals=rows * inner,
        ),
        compiler_params=pltpu.CompilerParams(vmem_limit_bytes=56 * 1024 * 1024),
    )(flag, first, second, *weights)


def finish(widened, scaling, gain_row, upstream, summed, forward_flag):
    forward_out = widened + summed
    scaled = summed * gain_row
    inner_mean = jnp.mean(scaled * widened, axis=-1, keepdims=True)
    cubed = scaling * scaling * scaling
    backward_out = upstream.astype(jnp.float32) + scaling * scaled - widened * cubed * inner_mean
    return jnp.where(forward_flag, forward_out, backward_out).astype(jnp.bfloat16)


def stack(blocks, chunk):
    return jnp.concatenate([blocks[k] for k in chunk], axis=0)


def after(first, then):
    return lax.optimization_barrier((first, then))


def returned(outcomes, weighings, code_sum):
    near, far = outcomes
    far_back = exchange(far)
    far_back, near = after(far_back, near)
    near_back = exchange(near)
    parts = dict(zip(CHUNKS[0], combine(weighings[0], near_back, [TOKENS] * len(CHUNKS[0]))))
    *rest, first, last = combine(
        weighings[1], far_back, [TOKENS] * (len(CHUNKS[1]) - 1) + [TOKENS // 2] * 2
    )
    parts.update(zip(CHUNKS[1], (*rest, (first, last))))
    return sum_ring(parts) / code_sum


def body(boundary, saved, norm_gain, gate_weight, up_weight, down_weight, routes, gate_codes):
    first_segment = lax.axis_index("segment") == 0
    later_forward = jnp.logical_not(first_segment)
    width = boundary.shape[2]
    weights = (gate_weight[0, 0], up_weight[0, 0], down_weight[0, 0])
    gain_row = norm_gain[0]
    edge_rows = boundary[0]
    stored = saved[0]
    route_now = jnp.where(first_segment, routes[0, 0], routes[0, 1])
    codes_now = jnp.where(first_segment, gate_codes[0, 0], gate_codes[0, 1])
    route_next = jnp.where(first_segment, routes[0, 1], routes[0, 0])
    codes_next = jnp.where(first_segment, gate_codes[0, 1], gate_codes[0, 0])
    sum_now = jnp.sum(codes_now.astype(jnp.float32), axis=-1, keepdims=True)
    sum_next = jnp.sum(codes_next.astype(jnp.float32), axis=-1, keepdims=True)
    top = route_now.shape[1]
    info = jnp.concatenate((route_now, codes_now, route_next, codes_next), axis=1)
    info = jnp.pad(info.astype(jnp.bfloat16), ((0, 0), (0, 128 - 4 * top)))

    inputs_now = jnp.where(first_segment, edge_rows, stored)
    widened, scaling, _ = normalize(inputs_now, gain_row)

    forward_first = first_segment.astype(jnp.int32).reshape(1)
    told = jnp.stack((lax.axis_index(RING), first_segment.astype(jnp.int32)))

    blocks = gather_near(starting_block(forward_first, edge_rows, stored, gain_row, info))
    pairs, place_next, weigh_now, weigh_next = [], [], [], []
    for chunk in CHUNKS:
        if pairs:
            blocks = gather_far(blocks)
        picked, pick_next, by_now, by_next = pick_both(
            told, [blocks[k] for k in chunk], top, width
        )
        if pairs:
            pairs[-1], picked = after(pairs[-1], picked)
        else:
            picked, blocks = after(picked, blocks)
        pairs.append(exchange(picked))
        place_next.append(pick_next)
        weigh_now.append(by_now)
        weigh_next.append(by_next)
    outcomes = [apply_expert(forward_first, pair, 0, pair, 1, 0, weights) for pair in pairs]
    summed = returned(outcomes, weigh_now, sum_now)
    produced = finish(widened, scaling, gain_row, edge_rows, summed, first_segment)

    arrived = lax.ppermute(produced, "segment", [(0, 1), (1, 0)])
    inputs_next = jnp.where(first_segment, stored, arrived)
    widened_next, scaling_next, normed_next = normalize(inputs_next, gain_row)
    member_blocks = gather_far(gather_near(jnp.where(first_segment, arrived, normed_next)))
    landed = []
    for i, chunk in enumerate(CHUNKS):
        picked = pick(place_next[i], stack(member_blocks, chunk))
        if landed:
            landed[-1], picked = after(landed[-1], picked)
        landed.append(exchange(picked))
    outcomes = [
        apply_expert(1 - forward_first, pair, 1, rows, 0, 1, weights)
        for pair, rows in zip(pairs, landed)
    ]
    summed = returned(outcomes, weigh_next, sum_next)
    result = finish(widened_next, scaling_next, gain_row, arrived, summed, later_forward)
    return result[None]


def solution(mesh):
    finer = Mesh(
        mesh.devices.reshape(mesh.shape["segment"], 4, 2, 8, 2),
        ("segment", "expert_0", "expert_1", "expert_2", "expert_3"),
    )
    placed = (
        P("segment", EXPERT, None),
        P("segment", EXPERT, None),
        P("segment", None),
        P("segment", EXPERT, None, None),
        P("segment", EXPERT, None, None),
        P("segment", EXPERT, None, None),
        P("segment", None, EXPERT, None),
        P("segment", None, EXPERT, None),
    )
    return jax.shard_map(
        body, mesh=finer, in_specs=placed, out_specs=P("segment", EXPERT, None), check_vma=False
    )
```

```python
import functools

import jax
import jax.numpy as jnp
from jax import lax
from jax.experimental import pallas as pl
from jax.experimental.pallas import tpu as pltpu
from jax.sharding import Mesh
from jax.sharding import PartitionSpec as P

EXPERT = ("expert_0", "expert_1", "expert_2", "expert_3")
PLANE = ("expert_0", "expert_1", "expert_3")
RING = "expert_2"

CHUNKS = ((0, -1, 1, -2), (2, -3, 3, 4))
CAPACITY = 6
TOKENS = 64

epsilon = 1e-06


def step_ring(block, step):
    count = lax.axis_size(RING)
    return lax.ppermute(block, RING, [(i, (i + step) % count) for i in range(count)])


def gather_near(own):
    blocks = {0: own}
    for distance in (1, 2):
        blocks[-distance] = step_ring(blocks[1 - distance], 1)
        blocks[distance] = step_ring(blocks[distance - 1], -1)
    return blocks


def gather_far(blocks):
    half = blocks[0].shape[0] // 2
    up, down = step_ring(blocks[-2], 1), step_ring(blocks[2], -1)
    last = jnp.concatenate((step_ring(up[:half], 1), step_ring(down[half:], -1)), axis=0)
    return {**blocks, -3: up, 3: down, 4: last}


def add(part, arrived):
    return (part.astype(jnp.float32) + arrived.astype(jnp.float32)).astype(jnp.bfloat16)


def sum_ring(parts):
    first, last = parts[4]
    half = first.shape[0]
    up, down = step_ring(first, 1), step_ring(last, -1)
    up = jnp.concatenate((add(parts[3][:half], up), parts[3][half:]), axis=0)
    down = jnp.concatenate((parts[-3][:half], add(parts[-3][half:], down)), axis=0)
    for distance in (2, 1):
        up = add(parts[distance], step_ring(up, 1))
        down = add(parts[-distance], step_ring(down, -1))
    up, down = step_ring(up, 1), step_ring(down, -1)
    return sum(part.astype(jnp.float32) for part in (parts[0], up, down))


def exchange(rows):
    count = lax.axis_size(PLANE)
    parts = rows.reshape(count, -1, rows.shape[-1])
    moved = lax.all_to_all(parts, PLANE, split_axis=0, concat_axis=0, tiled=True)
    return moved.reshape(rows.shape)


def one_hots(ids, codes, first_chip, ring, peers):
    width = ids.shape[1]
    blocks = width // TOKENS
    plane = lax.broadcasted_iota(jnp.int32, (peers, 1), 0)
    named = ((((plane >> 1) * ring + first_chip) << 1) + (plane & 1)).astype(jnp.float32)
    member = jnp.zeros((peers, width), jnp.float32)
    code = jnp.zeros((peers, width), jnp.float32)
    for k in range(ids.shape[0]):
        hit = ids[k : k + 1, :] == named
        member = jnp.where(hit, 1.0, member)
        code = jnp.where(hit, codes[k : k + 1, :], code)
    row = lax.broadcasted_iota(jnp.int32, (width, width), 0)
    column = lax.broadcasted_iota(jnp.int32, (width, width), 1)
    earlier = jnp.where((row // TOKENS == column // TOKENS) & (row < column), 1.0, 0.0)
    rank = jnp.dot(
        member.astype(jnp.bfloat16),
        earlier.astype(jnp.bfloat16),
        preferred_element_type=jnp.float32,
    )
    block = lax.broadcasted_iota(jnp.int32, (1, width), 1) // TOKENS
    key = jnp.where(member > 0.0, (block * CAPACITY).astype(jnp.float32) + rank, -1.0)
    rows = blocks * CAPACITY
    place = lax.broadcasted_iota(jnp.int32, (peers, rows, width), 1).astype(jnp.float32)
    found = jnp.broadcast_to(key[:, None, :], (peers, rows, width)) == place
    picking = jnp.where(found, 1.0, 0.0)
    weighing = jnp.where(found, jnp.broadcast_to(code[:, None, :], (peers, rows, width)), 0.0)
    return (picking.reshape(-1, width), weighing.reshape(-1, width))


def pick_kernel(top, ring, peers, told, *refs):
    count = len(refs) - 5
    blocks, (picked, next_out, by_now_out, by_next_out, held) = refs[:count], refs[count:]
    width = picked.shape[1] // 2
    for i, block in enumerate(blocks):
        held[i * TOKENS : (i + 1) * TOKENS, :] = block[...]
    info = jnp.transpose(held[:, 2 * width :].astype(jnp.float32))
    ids_now, codes_now, ids_next, codes_next = (info[i * top : (i + 1) * top, :] for i in range(4))
    pick_now, by_now = one_hots(ids_now, codes_now, told[0], ring, peers)
    pick_next, by_next = one_hots(ids_next, codes_next, told[0], ring, peers)
    early = jnp.where(told[1] == 1, pick_next, pick_now).astype(jnp.bfloat16)
    pick_now = pick_now.astype(jnp.bfloat16)
    picked[:, :width] = jnp.dot(
        pick_now, held[:, :width], preferred_element_type=jnp.float32
    ).astype(jnp.bfloat16)
    picked[:, width:] = jnp.dot(
        early, held[:, width : 2 * width], preferred_element_type=jnp.float32
    ).astype(jnp.bfloat16)
    next_out[...] = pick_next.astype(jnp.bfloat16)
    by_now_out[...] = by_now.astype(jnp.bfloat16)
    by_next_out[...] = by_next.astype(jnp.bfloat16)


def pick_both(told, blocks, top, width):
    ring, peers = lax.axis_size(RING), lax.axis_size(PLANE)
    tokens = len(blocks) * TOKENS
    rows = peers * len(blocks) * CAPACITY
    whole = pl.BlockSpec(memory_space=pltpu.VMEM)
    kept = pltpu.HBM((rows, tokens), jnp.bfloat16)
    blocks = [pltpu.with_memory_space_constraint(block, pltpu.HBM) for block in blocks]
    return pl.pallas_call(
        functools.partial(pick_kernel, top, ring, peers),
        in_specs=[pl.BlockSpec(memory_space=pltpu.SMEM)] + [whole] * len(blocks),
        out_specs=[whole] * 4,
        out_shape=[pltpu.HBM((rows, 2 * width), jnp.bfloat16), kept, kept, kept],
        scratch_shapes=[pltpu.VMEM((tokens, blocks[0].shape[1]), jnp.bfloat16)],
        cost_estimate=pl.CostEstimate(
            flops=4 * rows * tokens * width,
            bytes_accessed=4 * width * (tokens + rows) + 6 * rows * tokens,
            transcendentals=0,
        ),
        compiler_params=pltpu.CompilerParams(vmem_limit_bytes=32 * 1024 * 1024),
    )(told, *blocks)


def pick(picking, tokens):
    return jnp.dot(picking, tokens, preferred_element_type=jnp.float32).astype(jnp.bfloat16)


def combine_kernel(weighing, rows, *outs):
    total = jnp.dot(
        jnp.transpose(weighing[...]), rows[...], preferred_element_type=jnp.float32
    ).astype(jnp.bfloat16)
    at = 0
    for out in outs:
        out[...] = total[at : at + out.shape[0], :]
        at += out.shape[0]


def combine(weighing, rows, heights):
    whole = pl.BlockSpec(memory_space=pltpu.VMEM)
    return pl.pallas_call(
        combine_kernel,
        in_specs=[whole] * 2,
        out_specs=[whole] * len(heights),
        out_shape=[pltpu.HBM((height, rows.shape[1]), jnp.bfloat16) for height in heights],
        cost_estimate=pl.CostEstimate(
            flops=2 * weighing.size * rows.shape[1],
            bytes_accessed=2 * (weighing.size + rows.size + sum(heights) * rows.shape[1]),
            transcendentals=0,
        ),
        compiler_params=pltpu.CompilerParams(vmem_limit_bytes=24 * 1024 * 1024),
    )(weighing, rows)


def start_kernel(forward, edge, stored, gain, info, out):
    width = edge.shape[1]
    kept = stored[...].astype(jnp.float32)
    kept_scale = lax.rsqrt(jnp.mean(kept * kept, axis=-1, keepdims=True) + epsilon)
    kept = (kept * kept_scale * gain[...]).astype(jnp.bfloat16)
    out[:, 2 * width :] = info[...]

    @pl.when(forward[0] == 1)
    def _():
        fresh = edge[...].astype(jnp.float32)
        scale = lax.rsqrt(jnp.mean(fresh * fresh, axis=-1, keepdims=True) + epsilon)
        out[:, :width] = (fresh * scale * gain[...]).astype(jnp.bfloat16)
        out[:, width : 2 * width] = kept

    @pl.when(forward[0] != 1)
    def _():
        out[:, :width] = kept
        out[:, width : 2 * width] = edge[...]


def starting_block(forward, edge, stored, gain, info):
    whole = pl.BlockSpec(memory_space=pltpu.VMEM)
    tokens, width = edge.shape
    edge, stored = (pltpu.with_memory_space_constraint(rows, pltpu.HBM) for rows in (edge, stored))
    return pl.pallas_call(
        start_kernel,
        in_specs=[pl.BlockSpec(memory_space=pltpu.SMEM)] + [whole] * 4,
        out_specs=whole,
        out_shape=pltpu.HBM((tokens, 2 * width + info.shape[1]), jnp.bfloat16),
        compiler_params=pltpu.CompilerParams(vmem_limit_bytes=16 * 1024 * 1024),
    )(forward, edge, stored, gain.reshape(1, -1), info)


def normalize(inputs, gain_row):
    widened = inputs.astype(jnp.float32)
    scaling = lax.rsqrt(jnp.mean(widened * widened, axis=-1, keepdims=True) + epsilon)
    return (widened, scaling, (widened * scaling * gain_row).astype(jnp.bfloat16))


def transposed(left, right):
    return lax.dot_general(
        left, right, (((1,), (1,)), ((), ())), preferred_element_type=jnp.float32
    )


def expert_kernel(
    first_at, second_at, forward_from, flag, first, second, w_gate, w_up, w_down, out, *scratch
):
    first_rows, second_rows, gate, up, down, made, done = scratch
    rows, width = first_rows.shape
    into = (
        (first.at[:, pl.ds(first_at * width, width)], first_rows),
        (second.at[:, pl.ds(second_at * width, width)], second_rows),
        (w_gate, gate),
        (w_up, up),
        (w_down, down),
    )
    copies = [
        pltpu.make_async_copy(source, target, done.at[i]) for i, (source, target) in enumerate(into)
    ]
    for copy in (copies[0], copies[2], copies[3]):
        copy.start()
    for copy in (copies[0], copies[2]):
        copy.wait()
    for copy in (copies[1], copies[4]):
        copy.start()
    forward = flag[0] == 1
    piece = width // 4
    given = [
        pltpu.make_async_copy(made.at[:, part], out.at[:, part], done.at[5 + i])
        for i, part in enumerate(pl.ds(i * piece, piece) for i in range(4))
    ]

    @pl.when(forward)
    def _():
        copies[1].wait()
        taken = (first_rows, second_rows)[forward_from][...]
        gate_part = jnp.dot(taken, gate[...], preferred_element_type=jnp.float32)
        copies[3].wait()
        up_part = jnp.dot(taken, up[...], preferred_element_type=jnp.float32)
        hidden = (gate_part * jax.nn.sigmoid(gate_part) * up_part).astype(jnp.bfloat16)
        copies[4].wait()
        for i, copy in enumerate(given):
            part = slice(i * piece, (i + 1) * piece)
            total = jnp.dot(hidden, down[:, part], preferred_element_type=jnp.float32)
            made[:, part] = total.astype(jnp.bfloat16)
            copy.start()

    @pl.when(jnp.logical_not(forward))
    def _():
        taken = first_rows[...]
        gate_part = jnp.dot(taken, gate[...], preferred_element_type=jnp.float32)
        copies[3].wait()
        up_part = jnp.dot(taken, up[...], preferred_element_type=jnp.float32)
        copies[1].wait()
        copies[4].wait()
        hidden_grad = transposed(second_rows[...], down[...])
        sigmoid_part = jax.nn.sigmoid(gate_part)
        activated = gate_part * sigmoid_part
        slope = sigmoid_part * (1.0 + gate_part * (1.0 - sigmoid_part))
        gate_grad = (hidden_grad * up_part * slope).astype(jnp.bfloat16)
        up_grad = (hidden_grad * activated).astype(jnp.bfloat16)
        for i, copy in enumerate(given):
            part = slice(i * piece, (i + 1) * piece)
            total = transposed(gate_grad, gate[part, :]) + transposed(up_grad, up[part, :])
            made[:, part] = total.astype(jnp.bfloat16)
            copy.start()

    for copy in given:
        copy.wait()


def apply_expert(flag, first, first_at, second, second_at, forward_from, weights):
    rows, (width, inner) = first.shape[0], weights[0].shape
    weights = [pltpu.with_memory_space_constraint(w, pltpu.HBM) for w in weights]
    return pl.pallas_call(
        functools.partial(expert_kernel, first_at, second_at, forward_from),
        in_specs=[pl.BlockSpec(memory_space=pltpu.SMEM)] + [pl.BlockSpec(memory_space=pl.ANY)] * 5,
        out_specs=pl.BlockSpec(memory_space=pl.ANY),
        out_shape=pltpu.HBM((rows, width), jnp.bfloat16),
        scratch_shapes=[pltpu.VMEM((rows, width), jnp.bfloat16)] * 2
        + [pltpu.VMEM(w.shape, w.dtype) for w in weights]
        + [pltpu.VMEM((rows, width), jnp.bfloat16), pltpu.SemaphoreType.DMA((9,))],
        cost_estimate=pl.CostEstimate(
            flops=10 * rows * width * inner,
            bytes_accessed=6 * width * (rows + inner),
            transcendentals=rows * inner,
        ),
        compiler_params=pltpu.CompilerParams(vmem_limit_bytes=56 * 1024 * 1024),
    )(flag, first, second, *weights)


def finish(widened, scaling, gain_row, upstream, summed, forward_flag):
    forward_out = widened + summed
    scaled = summed * gain_row
    inner_mean = jnp.mean(scaled * widened, axis=-1, keepdims=True)
    cubed = scaling * scaling * scaling
    backward_out = upstream.astype(jnp.float32) + scaling * scaled - widened * cubed * inner_mean
    return jnp.where(forward_flag, forward_out, backward_out).astype(jnp.bfloat16)


def stack(blocks, chunk):
    return jnp.concatenate([blocks[k] for k in chunk], axis=0)


def after(first, then):
    return lax.optimization_barrier((first, then))


def returned(outcomes, weighings, code_sum):
    near, far = outcomes
    far_back = exchange(far)
    far_back, near = after(far_back, near)
    near_back = exchange(near)
    parts = dict(zip(CHUNKS[0], combine(weighings[0], near_back, [TOKENS] * len(CHUNKS[0]))))
    *rest, first, last = combine(
        weighings[1], far_back, [TOKENS] * (len(CHUNKS[1]) - 1) + [TOKENS // 2] * 2
    )
    parts.update(zip(CHUNKS[1], (*rest, (first, last))))
    return sum_ring(parts) / code_sum


def body(boundary, saved, norm_gain, gate_weight, up_weight, down_weight, routes, gate_codes):
    first_segment = lax.axis_index("segment") == 0
    later_forward = jnp.logical_not(first_segment)
    width = boundary.shape[2]
    weights = (gate_weight[0, 0], up_weight[0, 0], down_weight[0, 0])
    gain_row = norm_gain[0]
    edge_rows = boundary[0]
    stored = saved[0]
    route_now = jnp.where(first_segment, routes[0, 0], routes[0, 1])
    codes_now = jnp.where(first_segment, gate_codes[0, 0], gate_codes[0, 1])
    route_next = jnp.where(first_segment, routes[0, 1], routes[0, 0])
    codes_next = jnp.where(first_segment, gate_codes[0, 1], gate_codes[0, 0])
    sum_now = jnp.sum(codes_now.astype(jnp.float32), axis=-1, keepdims=True)
    sum_next = jnp.sum(codes_next.astype(jnp.float32), axis=-1, keepdims=True)
    top = route_now.shape[1]
    info = jnp.concatenate((route_now, codes_now, route_next, codes_next), axis=1)
    info = jnp.pad(info.astype(jnp.bfloat16), ((0, 0), (0, 128 - 4 * top)))

    inputs_now = jnp.where(first_segment, edge_rows, stored)
    widened, scaling, _ = normalize(inputs_now, gain_row)

    forward_first = first_segment.astype(jnp.int32).reshape(1)
    told = jnp.stack((lax.axis_index(RING), first_segment.astype(jnp.int32)))

    blocks = gather_near(starting_block(forward_first, edge_rows, stored, gain_row, info))
    pairs, place_next, weigh_now, weigh_next = [], [], [], []
    for chunk in CHUNKS:
        if pairs:
            blocks = gather_far(blocks)
        picked, pick_next, by_now, by_next = pick_both(
            told, [blocks[k] for k in chunk], top, width
        )
        if pairs:
            pairs[-1], picked = after(pairs[-1], picked)
        else:
            picked, blocks = after(picked, blocks)
        pairs.append(exchange(picked))
        place_next.append(pick_next)
        weigh_now.append(by_now)
        weigh_next.append(by_next)
    outcomes = [apply_expert(forward_first, pair, 0, pair, 1, 0, weights) for pair in pairs]
    summed = returned(outcomes, weigh_now, sum_now)
    produced = finish(widened, scaling, gain_row, edge_rows, summed, first_segment)

    arrived = lax.ppermute(produced, "segment", [(0, 1), (1, 0)])
    inputs_next = jnp.where(first_segment, stored, arrived)
    widened_next, scaling_next, normed_next = normalize(inputs_next, gain_row)
    member_blocks = gather_far(gather_near(jnp.where(first_segment, arrived, normed_next)))
    landed = []
    for i, chunk in enumerate(CHUNKS):
        picked = pick(place_next[i], stack(member_blocks, chunk))
        if landed:
            landed[-1], picked = after(landed[-1], picked)
        landed.append(exchange(picked))
    outcomes = [
        apply_expert(1 - forward_first, pair, 1, rows, 0, 1, weights)
        for pair, rows in zip(pairs, landed)
    ]
    summed = returned(outcomes, weigh_next, sum_next)
    result = finish(widened_next, scaling_next, gain_row, arrived, summed, later_forward)
    return result[None]


def solution(mesh):
    finer = Mesh(
        mesh.devices.reshape(mesh.shape["segment"], 4, 2, 8, 2),
        ("segment", "expert_0", "expert_1", "expert_2", "expert_3"),
    )
    placed = (
        P("segment", EXPERT, None),
        P("segment", EXPERT, None),
        P("segment", None),
        P("segment", EXPERT, None, None),
        P("segment", EXPERT, None, None),
        P("segment", EXPERT, None, None),
        P("segment", None, EXPERT, None),
        P("segment", None, EXPERT, None),
    )
    return jax.shard_map(
        body, mesh=finer, in_specs=placed, out_specs=P("segment", EXPERT, None), check_vma=False
    )
```
